32 devices in a mesh: dp: 8 (over z, x), tensor: 4 (over y, core).
Axes of the slice: x: 2, y: 2, z: 4, core: 2. Of those that a mesh axis runs over, the one named last changes fastest.
Arguments:
- inputs: bfloat16 [8192, 768], P(('dp', 'tensor')), may hold values from -6 to 6
- encoder: bfloat16 [4096, 768], P(('dp', 'tensor')), may hold values from -6 to 6
- buckets: int32 [1024, 1024], replicated, may hold values from 0 to 31
- query_weight: bfloat16 [1, 768, 768], P(None, 'dp', 'tensor'), may hold values from -0.0546875 to 0.0546875
- key_weight: bfloat16 [1, 768, 768], P(None, 'dp', 'tensor'), may hold values from -0.21875 to 0.21875
- value_weight: bfloat16 [1, 768, 768], P(None, 'dp', 'tensor'), may hold values from -0.21875 to 0.21875
- output_weight: bfloat16 [1, 768, 768], P(None, 'tensor', 'dp'), may hold values from -0.875 to 0.875
- crossquery: bfloat16 [1, 768, 768], P(None, 'dp', 'tensor'), may hold values from -0.0546875 to 0.0546875
- crosskey: bfloat16 [1, 768, 768], P(None, 'dp', 'tensor'), may hold values from -0.21875 to 0.21875
- crossvalue: bfloat16 [1, 768, 768], P(None, 'dp', 'tensor'), may hold values from -0.21875 to 0.21875
- crossoutput: bfloat16 [1, 768, 768], P(None, 'tensor', 'dp'), may hold values from -0.875 to 0.875
- gate_weight: bfloat16 [1, 768, 2048], P(None, 'dp', 'tensor'), may hold values from -0.21875 to 0.21875
- up_weight: bfloat16 [1, 768, 2048], P(None, 'dp', 'tensor'), may hold values from -0.21875 to 0.21875
- down_weight: bfloat16 [1, 2048, 768], P(None, 'tensor', 'dp'), may hold values from -0.125 to 0.125
- norm_gains: bfloat16 [1, 3, 768], replicated, may hold values from 0.5 to 1.5
- bias_table: bfloat16 [32, 12], replicated, may hold values from -4 to 4
- cotangent: bfloat16 [8192, 768], P(('dp', 'tensor')), may hold values from -6 to 6
Outputs:
- outputs: bfloat16 [8192, 768], P(('dp', 'tensor'))
- grad_inputs: float32 [8192, 768], P(('dp', 'tensor'))
- grad_encoder: float32 [4096, 768], P(('dp', 'tensor'))
- grad_query: float32 [1, 768, 768], P(None, 'dp', 'tensor')
- grad_key: float32 [1, 768, 768], P(None, 'dp', 'tensor')
- grad_value: float32 [1, 768, 768], P(None, 'dp', 'tensor')
- grad_output: float32 [1, 768, 768], P(None, 'tensor', 'dp')
- grad_crossquery: float32 [1, 768, 768], P(None, 'dp', 'tensor')
- grad_crosskey: float32 [1, 768, 768], P(None, 'dp', 'tensor')
- grad_crossvalue: float32 [1, 768, 768], P(None, 'dp', 'tensor')
- grad_crossoutput: float32 [1, 768, 768], P(None, 'tensor', 'dp')
- grad_gate: float32 [1, 768, 2048], P(None, 'dp', 'tensor')
- grad_up: float32 [1, 768, 2048], P(None, 'dp', 'tensor')
- grad_down: float32 [1, 2048, 768], P(None, 'tensor', 'dp')
- grad_gains: float32 [1, 3, 768], replicated
- grad_table: float32 [32, 12], replicated
The draws below stay inside these ranges and needn't reach their ends.
All inputs are finite; a program needn't handle non-finite values.
Results may differ from the reference program's by a relative error of at most 0.025.
The reference program's roundings to bfloat16 on the way count: a program that leaves them out, or rounds other values in their place, can miss the bound.
Values may be sent and summed in bfloat16 or wider, within the bound.
No kernel may reach another device: no remote copies, remote signals or barrier semaphores. Data moves between devices by JAX's collectives and lax.ppermute only.
A program may use at most 128 MiB of HBM per device.

```python
from functools import partial
import jax
import jax.numpy as jnp
from jax import lax

D = 768
HEADS = 12
HEAD_DIM = 64
FF = 2048
BUCKETS = 32
SEQ_LEN = 1024
ENC_LEN = 512
LAYERS = 1
TOKENS = 8192
SOURCES = 4096


def plant(values, rng, smallest, high):
    place = [jax.random.randint(jax.random.fold_in(rng, axis), (), 0, length) for axis, length in enumerate(values.shape)]
    longest = values.shape.index(max(values.shape))
    neighbour = place[:longest] + [(place[longest] + 1) % values.shape[longest]] + place[longest + 1:]
    return values.at[tuple(place)].set(smallest).at[tuple(neighbour)].set(high)


def spiked(entries, rng, source, target, parts, factor):
    def block_of(axis_at):
        return (jnp.arange(entries.shape[axis_at]) // (entries.shape[axis_at] // parts)).reshape((-1,) + (1,) * (entries.ndim - 1 - axis_at))

    first = jax.random.permutation(rng, parts)[block_of(target)]
    other_side = (block_of(target) + parts // 2) % parts
    return jnp.where((block_of(source) == first) | (block_of(source) == other_side), factor * entries, entries)


def levels(key, shape, shards, low, largest):
    def one(position, blocks):
        steps = jax.random.uniform(jax.random.fold_in(jax.random.fold_in(key, 6), position), (blocks,), jnp.float32, low / len(shards), largest / len(shards))
        return jnp.repeat(jnp.exp(steps), shape[position] // blocks).reshape((-1,) + (1,) * (len(shape) - position - 1))

    factor_of = one(*shards[0])
    for cut in shards[1:]:
        factor_of = factor_of * one(*cut)
    return factor_of


def gaussian(stream_key, extent, width, reach, cuts=(), dtype=jnp.bfloat16):
    loudness = levels(stream_key, extent, cuts, -0.22, 0.18) if cuts else 1.0
    array = jax.random.normal(stream_key, extent, jnp.float32) * width * loudness
    return jnp.minimum(jnp.maximum(array, -reach), reach).astype(dtype)


def gaussian_with(own_key, dims, width, most, cuts, heavy, dtype=jnp.bfloat16):
    drawn = width * jax.random.normal(own_key, dims, jnp.float32)
    if cuts:
        drawn = drawn * levels(own_key, dims, cuts, -0.22, 0.18)
    return jnp.clip(spiked(drawn, jax.random.fold_in(own_key, 3), *heavy), -most, most).astype(dtype)


def setup_inputs(seed: int = 0) -> dict:
    arg_keys = jax.random.split(jax.random.key(seed), 18)
    inputs = gaussian_with(arg_keys[0], (TOKENS, D), 1.0, 6.0, ((0, 32),), (0, 1, 32, 2.75))
    encoder = gaussian(arg_keys[1], (SOURCES, D), 1.0, 6.0, ((0, 32),))
    buckets = plant(jax.random.randint(arg_keys[2], (SEQ_LEN, SEQ_LEN), 0, BUCKETS), jax.random.fold_in(arg_keys[2], 1), 0, BUCKETS - 1).astype(jnp.int32)
    query_weight = gaussian(arg_keys[3], (LAYERS, D, HEADS * HEAD_DIM), (D * 16) ** -0.5, 0.0546875, ((1, 8), (2, 4)))
    key_weight = gaussian(arg_keys[4], (LAYERS, D, HEADS * HEAD_DIM), D ** -0.5, 0.21875, ((1, 8), (2, 4)))
    value_weight = gaussian(arg_keys[5], (LAYERS, D, HEADS * HEAD_DIM), D ** -0.5, 0.21875, ((1, 8), (2, 4)))
    output_weight = gaussian(arg_keys[6], (LAYERS, HEADS * HEAD_DIM, D), (HEADS * HEAD_DIM // 16) ** -0.5, 0.875, ((1, 4), (2, 8)))
    crossquery = gaussian(arg_keys[7], (LAYERS, D, HEADS * HEAD_DIM), (D * 16) ** -0.5, 0.0546875, ((1, 8), (2, 4)))
    crosskey = gaussian(arg_keys[8], (LAYERS, D, HEADS * HEAD_DIM), D ** -0.5, 0.21875, ((1, 8), (2, 4)))
    crossvalue = gaussian(arg_keys[9], (LAYERS, D, HEADS * HEAD_DIM), D ** -0.5, 0.21875, ((1, 8), (2, 4)))
    crossoutput = gaussian(arg_keys[10], (LAYERS, HEADS * HEAD_DIM, D), (HEADS * HEAD_DIM // 16) ** -0.5, 0.875, ((1, 4), (2, 8)))
    gate_weight = gaussian(arg_keys[11], (LAYERS, D, FF), D ** -0.5, 0.21875, ((1, 8), (2, 4)))
    up_weight = gaussian(arg_keys[12], (LAYERS, D, FF), D ** -0.5, 0.21875, ((1, 8), (2, 4)))
    down_weight = gaussian(arg_keys[13], (LAYERS, FF, D), FF ** -0.5, 0.125, ((1, 4), (2, 8)))
    norm_gains = jnp.clip(1.0 + 0.1 * jax.random.normal(arg_keys[14], (LAYERS, 3, D), jnp.float32), 0.5, 1.5).astype(jnp.bfloat16)
    bias_table = gaussian(arg_keys[15], (BUCKETS, HEADS), 1.0, 4.0)
    cotangent = gaussian(arg_keys[16], (TOKENS, D), 1.0, 6.0, ((0, 32),))
    return {"inputs": inputs, "encoder": encoder, "buckets": buckets, "query_weight": query_weight, "key_weight": key_weight, "value_weight": value_weight, "output_weight": output_weight, "crossquery": crossquery, "crosskey": crosskey, "crossvalue": crossvalue, "crossoutput": crossoutput, "gate_weight": gate_weight, "up_weight": up_weight, "down_weight": down_weight, "norm_gains": norm_gains, "bias_table": bias_table, "cotangent": cotangent}


@jax.custom_vjp
def low(v):
    return lax.optimization_barrier(v.astype(jnp.bfloat16)).astype(jnp.float32)

@jax.custom_vjp
def low_back(v):
    return v

def low_keep(v):
    return (low(v), None)

def low_pass(kept, grad):
    return (grad,)

def back_keep(v):
    return (v, None)

def back_low(kept, grad):
    return (low(grad),)
low.defvjp(low_keep, low_pass)
low_back.defvjp(back_keep, back_low)

def product(left, right):
    return jnp.dot(left, right, precision=lax.Precision.HIGHEST, preferred_element_type=jnp.float32)

def lowered(values):
    return low_back(low(values))

def normalize(values, gain_row):
    inverse_root = lax.rsqrt(lax.optimization_barrier(jnp.mean(values * values, axis=-1, keepdims=True)) + 1e-06)
    return values * inverse_root * gain_row

def attention(position_bias, causal, blocks):
    queries, key_rows, value_rows = blocks
    scores = low_back(jnp.einsum('qhd,khd->hqk', queries, key_rows, precision=lax.Precision.HIGHEST, preferred_element_type=jnp.float32))
    if causal:
        row_ids = jnp.arange(queries.shape[0])[:, None]
        column_ids = jnp.arange(key_rows.shape[0])[None, :]
        scores = jnp.where(column_ids <= row_ids, scores + position_bias, -1000000000.0)
    shares = jax.nn.softmax(scores, axis=-1)
    mixture = jnp.einsum('hqk,khd->qhd', low(shares), value_rows, precision=lax.Precision.HIGHEST, preferred_element_type=jnp.float32)
    return lowered(mixture.reshape(queries.shape[0], -1))

def split_heads(matrix, length):
    return matrix.reshape(-1, length, HEADS, HEAD_DIM)

def decoder_layer(residual, memory, matrices, gain_rows, position_bias):
    query_weight, key_weight, value_weight, output_weight, crossquery, crosskey, crossvalue, crossoutput, gate_weight, up_weight, down_weight = matrices
    token_count = residual.shape[0]
    normed = low(normalize(residual, gain_rows[0]))
    blocks = (split_heads(lowered(product(normed, query_weight)), SEQ_LEN), split_heads(lowered(product(normed, key_weight)), SEQ_LEN), split_heads(lowered(product(normed, value_weight)), SEQ_LEN))
    mixture = lax.map(jax.checkpoint(partial(attention, position_bias, True)), blocks)
    residual = residual + low_back(product(mixture.reshape(token_count, -1), output_weight))
    normed = low(normalize(residual, gain_rows[1]))
    blocks = (split_heads(lowered(product(normed, crossquery)), SEQ_LEN), split_heads(lowered(product(memory, crosskey)), ENC_LEN), split_heads(lowered(product(memory, crossvalue)), ENC_LEN))
    mixture = lax.map(jax.checkpoint(partial(attention, None, False)), blocks)
    residual = residual + low_back(product(mixture.reshape(token_count, -1), crossoutput))
    normed = low(normalize(residual, gain_rows[2]))
    gate_sums = low_back(product(normed, gate_weight))
    up_sums = low_back(product(normed, up_weight))
    hidden = low(jax.nn.gelu(gate_sums, approximate=True) * up_sums)
    return residual + low_back(product(hidden, down_weight))

def forward(residual, memory, matrices, gain_table, table_full, buckets):
    position_bias = jnp.moveaxis(table_full[buckets], 2, 0)
    for layer_index in range(LAYERS):
        layer_matrices = tuple((matrix[layer_index] for matrix in matrices))
        residual = decoder_layer(residual, memory, layer_matrices, gain_table[layer_index], position_bias)
    return residual

def reference(inputs, encoder, buckets, query_weight, key_weight, value_weight, output_weight, crossquery, crosskey, crossvalue, crossoutput, gate_weight, up_weight, down_weight, norm_gains, bias_table, cotangent):
    matrices = tuple((matrix.astype(jnp.float32) for matrix in (query_weight, key_weight, value_weight, output_weight, crossquery, crosskey, crossvalue, crossoutput, gate_weight, up_weight, down_weight)))
    gain_table = norm_gains.astype(jnp.float32)
    table_full = bias_table.astype(jnp.float32)
    per_group = 4
    group_count = TOKENS // (per_group * SEQ_LEN)
    token_rows = inputs.astype(jnp.float32).reshape(group_count, per_group * SEQ_LEN, D)
    memory_rows = encoder.astype(jnp.float32).reshape(group_count, per_group * ENC_LEN, D)
    grad_rows = cotangent.astype(jnp.float32).reshape(group_count, per_group * SEQ_LEN, D)

    def group_step(totals, pieces):
        residual, memory, upstream = pieces

        def run_forward(residual_in, memory_in, matrices_in, gains_in, table_in):
            return forward(residual_in, memory_in, matrices_in, gains_in, table_in, buckets)
        result, pullback = jax.vjp(run_forward, residual, memory, matrices, gain_table, table_full)
        gradients = pullback(upstream)
        totals = jax.tree.map(lambda current, update: current + update, totals, gradients[2:])
        return (totals, (result, gradients[0], gradients[1]))
    zero_sums = jax.tree.map(jnp.zeros_like, (matrices, gain_table, table_full))
    (matrix_grads, gain_grads, table_grads), (result, input_grads, memory_grads) = lax.scan(group_step, zero_sums, (token_rows, memory_rows, grad_rows))
    return (result.reshape(TOKENS, D).astype(jnp.bfloat16), input_grads.reshape(TOKENS, D), memory_grads.reshape(SOURCES, D), matrix_grads[0], matrix_grads[1], matrix_grads[2], matrix_grads[3], matrix_grads[4], matrix_grads[5], matrix_grads[6], matrix_grads[7], matrix_grads[8], matrix_grads[9], matrix_grads[10], gain_grads, table_grads)
```

```python
import jax
import jax.numpy as jnp
from jax import lax
from jax.experimental import pallas as pl
from jax.experimental.pallas import tpu as pltpu
from jax.sharding import PartitionSpec as P

HEADS = 12
HEAD_DIM = 64
EPS = 1e-06
BF = jnp.bfloat16
F32 = jnp.float32
BLOCK = 256
VMEM_LIMIT = 40 * 1024 * 1024

CORE = [(0, 1), (1, 0), (2, 3), (3, 2)]
CHIP = [(0, 2), (2, 0), (1, 3), (3, 1)]


def gather_rows(piece):
    far = lax.ppermute(piece, "tensor", CHIP)
    near = lax.ppermute(piece, "tensor", CORE)
    last = lax.ppermute(far, "tensor", CORE)
    return jnp.concatenate([piece, far, near, last])


def scatter_sums(partial):
    rows = partial.shape[0] // 4
    near = lax.ppermute(partial[2 * rows :], "tensor", CORE)
    sums = partial[: 2 * rows].astype(F32) + near.astype(F32)
    far = lax.ppermute(sums[rows:].astype(BF), "tensor", CHIP)
    return sums[:rows] + far.astype(F32)


def swap_pairs(size, bit):
    return [(i, i ^ bit) for i in range(size)]


def gather_weights(shard):
    size = lax.axis_size("dp")
    me = lax.axis_index("dp")
    held = shard
    axis = 1
    bit = size // 2
    while bit >= 1:
        other = lax.ppermute(held, "dp", swap_pairs(size, bit))
        second = (me & bit) != 0
        held = jnp.stack(
            [jnp.where(second, other, held), jnp.where(second, held, other)], axis=axis
        )
        axis += 1
        bit //= 2
    return held.reshape(shard.shape[0], -1, shard.shape[2])


def reduce_weights(grads):
    size = lax.axis_size("dp")
    me = lax.axis_index("dp")
    count, total, columns = grads.shape
    levels = size.bit_length() - 1
    current = grads.reshape((count,) + (2,) * levels + (total // size, columns))
    bit = 1
    while bit < size:
        axis = current.ndim - 3
        mine = jnp.where((me & bit) != 0, 1, 0)
        send = lax.dynamic_index_in_dim(current, 1 - mine, axis, keepdims=False).astype(BF)
        keep = lax.dynamic_index_in_dim(current, mine, axis, keepdims=False)
        received = lax.ppermute(send, "dp", swap_pairs(size, bit))
        current = keep.astype(F32) + received.astype(F32)
        bit *= 2
    return current


def sum_everywhere(values):
    for pairs in (CORE, CHIP):
        values = values + lax.ppermute(values, "tensor", pairs)
    size = lax.axis_size("dp")
    bit = 1
    while bit < size:
        values = values + lax.ppermute(values, "dp", swap_pairs(size, bit))
        bit *= 2
    return values


def dot_nn(left, right):
    return jnp.dot(left, right, preferred_element_type=F32)


def dot_nt(left, right):
    return lax.dot_general(left, right, (((1,), (1,)), ((), ())), preferred_element_type=F32)


def dot_tn(left, right):
    return lax.dot_general(left, right, (((0,), (0,)), ((), ())), preferred_element_type=F32)


def normalize(values, gain_row):
    inverse_root = lax.rsqrt(jnp.mean(values * values, axis=-1, keepdims=True) + EPS)
    return values * inverse_root * gain_row


def normalize_back(values, gain_row, grad):
    inverse_root = lax.rsqrt(jnp.mean(values * values, axis=-1, keepdims=True) + EPS)
    scaled = values * inverse_root
    gain_grad = jnp.sum(grad * scaled, axis=0)
    inner = grad * gain_row
    back = inverse_root * (inner - scaled * jnp.mean(inner * scaled, axis=-1, keepdims=True))
    return back, gain_grad


def row_place(block, here):
    turned = lax.bitwise_xor(block, here)
    return lax.bitwise_or(
        lax.shift_left(lax.bitwise_and(turned, 1), 1), lax.shift_right_logical(turned, 1)
    )


def head_masks(rows, columns):
    lane_head = lax.broadcasted_iota(jnp.int32, (rows, columns), 1) // HEAD_DIM
    return [lane_head == head for head in range(columns // HEAD_DIM)]


def only(mask, values):
    return jnp.where(mask, values, jnp.zeros_like(values))


def call(kernel, name, grid, in_specs, out_specs, out_shape, scratch, flops, moved, args, scalars=1):
    return pl.pallas_call(
        kernel,
        grid_spec=pltpu.PrefetchScalarGridSpec(
            num_scalar_prefetch=scalars,
            grid=grid,
            in_specs=in_specs,
            out_specs=out_specs,
            scratch_shapes=scratch,
        ),
        out_shape=out_shape,
        compiler_params=pltpu.CompilerParams(
            dimension_semantics=("arbitrary",) * len(grid), vmem_limit_bytes=VMEM_LIMIT
        ),
        cost_estimate=pl.CostEstimate(flops=flops, bytes_accessed=moved, transcendentals=0),
        name=name,
    )(*args)


def whole(shape):
    return pl.BlockSpec(shape, lambda i, s: (0,) * len(shape))


def member(index, shape):
    return pl.BlockSpec((None,) + shape, lambda i, s: (index,) + (0,) * len(shape))


def bias_kernel(here_ref, buckets_ref, table_ref, bias_ref, low_ref):
    block = pl.program_id(0)
    heads = bias_ref.shape[0]
    length = buckets_ref.shape[1]
    for column in range(length // 128):

        @pl.when(column * 128 < (block + 1) * BLOCK)
        def _():
            lanes = slice(column * 128, (column + 1) * 128)
            ids = buckets_ref[:, lanes]
            low_ref[:, lanes] = ids.astype(F32).astype(BF)
            for head in range(heads):
                row = jnp.broadcast_to(table_ref[head : head + 1, :], ids.shape)
                picked = jnp.take_along_axis(row, ids, axis=1, mode="promise_in_bounds")
                bias_ref[head, :, lanes] = picked.astype(BF)


def make_bias(here, buckets, table_rows, heads):
    length = buckets.shape[0]
    blocks = length // BLOCK
    return call(
        bias_kernel,
        "position_bias",
        (blocks,),
        [pl.BlockSpec((BLOCK, length), lambda i, s: (i, 0)), whole(table_rows.shape)],
        [
            pl.BlockSpec((heads, BLOCK, length), lambda i, s: (0, i, 0)),
            pl.BlockSpec((BLOCK, length), lambda i, s: (i, 0)),
        ],
        [
            jax.ShapeDtypeStruct((heads, length, length), BF),
            jax.ShapeDtypeStruct((length, length), BF),
        ],
        [],
        0,
        12 * length * length,
        (here, buckets, table_rows),
    )


def self_kernel(here_ref, rows_ref, w_ref, bias_ref, q_ref, k_ref, v_ref, share_ref, mix_ref):
    block = pl.program_id(0)
    here = here_ref[0]
    length = rows_ref.shape[0]
    width = q_ref.shape[1]
    masks = head_masks(BLOCK, width)

    @pl.when(block == 0)
    def _():
        def project(index, _):
            place = pl.ds(pl.multiple_of(index * BLOCK, BLOCK), BLOCK)
            rows = rows_ref[place, :]
            for number, target in enumerate((q_ref, k_ref, v_ref)):
                target[place, :] = dot_nn(rows, w_ref[number]).astype(BF)
            return 0

        lax.fori_loop(0, length // BLOCK, project, 0)

    def one(index):
        def at(quarter):
            return pl.ds(pl.multiple_of(row_place(quarter, here) * BLOCK, BLOCK), BLOCK)

        queries = q_ref[at(index), :]
        keys = [k_ref[at(other), :] for other in range(index + 1)]
        values = [v_ref[at(other), :] for other in range(index + 1)]
        visible = lax.broadcasted_iota(jnp.int32, (BLOCK, BLOCK), 1) <= lax.broadcasted_iota(
            jnp.int32, (BLOCK, BLOCK), 0
        )
        mixture = jnp.zeros((BLOCK, width), F32)
        for head, mask in enumerate(masks):
            own = only(mask, queries)
            scores = []
            for other in range(index + 1):
                lanes = slice(other * BLOCK, (other + 1) * BLOCK)
                score = dot_nt(own, keys[other]) + bias_ref[head, :, lanes].astype(F32)
                if other == index:
                    score = jnp.where(visible, score, -1000000000.0)
                scores.append(score)
            highest = scores[0]
            for score in scores[1:]:
                highest = jnp.maximum(highest, score)
            highest = jnp.max(highest, axis=-1, keepdims=True)
            raised = [jnp.exp(score - highest) for score in scores]
            total = raised[0]
            for part in raised[1:]:
                total = total + part
            inverse = 1.0 / jnp.sum(total, axis=-1, keepdims=True)
            mixed = None
            for other in range(index + 1):
                lanes = slice(other * BLOCK, (other + 1) * BLOCK)
                share = (raised[other] * inverse).astype(BF)
                share_ref[head, :, lanes] = share
                part = dot_nn(share, values[other])
                mixed = part if mixed is None else mixed + part
            mixture = mixture + only(mask, mixed)
        mix_ref[...] = mixture.astype(BF)

    for index in range(length // BLOCK):
        pl.when(block == index)(lambda index=index: one(index))


def self_forward(here, rows, weights, bias):
    length, width = rows.shape
    heads = bias.shape[0]
    columns = weights.shape[2]
    blocks = length // BLOCK
    whole_rows = jax.ShapeDtypeStruct((length, columns), BF)
    return call(
        self_kernel,
        "self_forward",
        (blocks,),
        [
            whole((length, width)),
            whole(weights.shape),
            pl.BlockSpec((heads, BLOCK, length), lambda i, s: (0, i, 0)),
        ],
        [
            whole((length, columns)),
            whole((length, columns)),
            whole((length, columns)),
            pl.BlockSpec((heads, BLOCK, length), lambda i, s: (0, i, 0)),
            pl.BlockSpec((BLOCK, columns), lambda i, s: (row_place(i, s[0]), 0)),
        ],
        [
            whole_rows,
            whole_rows,
            whole_rows,
            jax.ShapeDtypeStruct((heads, length, length), BF),
            whole_rows,
        ],
        [],
        2 * length * width * columns * 3 + 4 * heads * length * length * HEAD_DIM * 4,
        16 * length * length,
        (here, rows, weights, bias),
    )


def cross_kernel(here_ref, rows_ref, w_ref, k_ref, v_ref, q_ref, share_ref, mix_ref):
    width = q_ref.shape[1]
    masks = head_masks(BLOCK, width)
    queries = dot_nn(rows_ref[...], w_ref[...]).astype(BF)
    q_ref[...] = queries
    keys = k_ref[...]
    values = v_ref[...]
    mixture = jnp.zeros((BLOCK, width), F32)
    for head, mask in enumerate(masks):
        scores = dot_nt(only(mask, queries), keys)
        raised = jnp.exp(scores - jnp.max(scores, axis=-1, keepdims=True))
        share = (raised * (1.0 / jnp.sum(raised, axis=-1, keepdims=True))).astype(BF)
        share_ref[head] = share
        mixture = mixture + only(mask, dot_nn(share, values))
    mix_ref[...] = mixture.astype(BF)


def cross_forward(here, rows, weights, keys, values):
    length, width = rows.shape
    columns = weights.shape[2]
    heads = columns // HEAD_DIM
    sources = keys.shape[0]
    blocks = length // BLOCK
    whole_rows = jax.ShapeDtypeStruct((length, columns), BF)
    row_spec = pl.BlockSpec((BLOCK, columns), lambda i, s: (i, 0))
    return call(
        cross_kernel,
        "cross_forward",
        (blocks,),
        [
            pl.BlockSpec((BLOCK, width), lambda i, s: (i, 0)),
            member(1, (width, columns)),
            whole((sources, columns)),
            whole((sources, columns)),
        ],
        [row_spec, pl.BlockSpec((heads, BLOCK, sources), lambda i, s: (0, i, 0)), row_spec],
        [whole_rows, jax.ShapeDtypeStruct((heads, length, sources), BF), whole_rows],
        [],
        2 * length * width * columns + 16 * heads * length * sources * HEAD_DIM,
        8 * length * length,
        (here, rows, weights, keys, values),
    )


def ff_kernel(here_ref, rows_ref, w_ref, grad_ref, hidden_ref, grad_gate_ref, grad_up_ref, dn_ref):
    rows = rows_ref[...]
    gate = dot_nn(rows, w_ref[0])
    up = dot_nn(rows, w_ref[1])
    grad = grad_ref[...]
    slope = 0.7978845608028654
    square = gate * gate
    bent = jnp.tanh(slope * (gate + 0.044715 * (square * gate)))
    half = 0.5 * (1.0 + bent)
    active = gate * half
    change = half + 0.5 * gate * (1.0 - bent * bent) * slope * (1.0 + 3.0 * 0.044715 * square)
    hidden_ref[...] = (active * up).astype(BF)
    grad_gate = (grad * up * change).astype(BF)
    grad_up = (grad * active).astype(BF)
    grad_gate_ref[...] = grad_gate
    grad_up_ref[...] = grad_up
    dn_ref[...] = (dot_nt(grad_gate, w_ref[0]) + dot_nt(grad_up, w_ref[1])).astype(BF)


def feed_forward(here, rows, weights, grad):
    length, width = rows.shape
    columns = weights.shape[2]
    blocks = length // BLOCK
    row_spec = pl.BlockSpec((BLOCK, columns), lambda i, s: (i, 0))
    whole_rows = jax.ShapeDtypeStruct((length, columns), BF)
    return call(
        ff_kernel,
        "feed_forward",
        (blocks,),
        [
            pl.BlockSpec((BLOCK, width), lambda i, s: (i, 0)),
            pl.BlockSpec((2, width, columns), lambda i, s: (0, 0, 0)),
            row_spec,
        ],
        [row_spec, row_spec, row_spec, pl.BlockSpec((BLOCK, width), lambda i, s: (i, 0))],
        [whole_rows, whole_rows, whole_rows, jax.ShapeDtypeStruct((length, width), BF)],
        [],
        8 * length * width * columns,
        12 * length * width,
        (here, rows, weights, grad),
    )


def cross_back_kernel(
    here_ref, grad_ref, w_out_ref, w_q_ref, share_ref, q_ref, k_ref, v_ref,
    dq_ref, dkv_ref, dn_ref, dk_sum, dv_sum,
):
    block = pl.program_id(0)
    width = q_ref.shape[1]
    masks = head_masks(BLOCK, width)
    grad = dot_nn(grad_ref[...], w_out_ref[...]).astype(BF)
    queries = q_ref[...]
    keys = k_ref[...]
    values = v_ref[...]

    @pl.when(block == 0)
    def _():
        dk_sum[...] = jnp.zeros_like(dk_sum)
        dv_sum[...] = jnp.zeros_like(dv_sum)

    dq = jnp.zeros((BLOCK, width), F32)
    dk = dk_sum[...]
    dv = dv_sum[...]
    for head, mask in enumerate(masks):
        own_grad = only(mask, grad)
        low = share_ref[head]
        share = low.astype(F32)
        weighted = dot_nt(own_grad, values) * share
        inner = jnp.sum(weighted, axis=-1, keepdims=True)
        grad_low = (weighted - share * inner).astype(BF)
        dq = dq + only(mask, dot_nn(grad_low, keys))
        dk = dk + dot_tn(grad_low, only(mask, queries))
        dv = dv + dot_tn(low, own_grad)
    dk_sum[...] = dk
    dv_sum[...] = dv
    dq = dq.astype(BF)
    dq_ref[...] = dq
    dn_ref[...] = dot_nt(dq, w_q_ref[...]).astype(BF)

    @pl.when(block == pl.num_programs(0) - 1)
    def _():
        dkv_ref[0] = dk.astype(BF)
        dkv_ref[1] = dv.astype(BF)


def cross_backward(here, grad, weights, shares, queries, keys, values):
    length, width = grad.shape
    columns = weights.shape[2]
    heads = columns // HEAD_DIM
    sources = keys.shape[0]
    blocks = length // BLOCK
    row_spec = pl.BlockSpec((BLOCK, columns), lambda i, s: (i, 0))
    wide_spec = pl.BlockSpec((BLOCK, width), lambda i, s: (i, 0))
    return call(
        cross_back_kernel,
        "cross_backward",
        (blocks,),
        [
            wide_spec,
            member(4, (width, columns)),
            member(1, (width, columns)),
            pl.BlockSpec((heads, BLOCK, sources), lambda i, s: (0, i, 0)),
            row_spec,
            whole((sources, columns)),
            whole((sources, columns)),
        ],
        [row_spec, whole((2, sources, columns)), wide_spec],
        [
            jax.ShapeDtypeStruct((length, columns), BF),
            jax.ShapeDtypeStruct((2, sources, columns), BF),
            jax.ShapeDtypeStruct((length, width), BF),
        ],
        [pltpu.VMEM((sources, columns), F32), pltpu.VMEM((sources, columns), F32)],
        4 * length * width * columns + 32 * heads * length * sources * HEAD_DIM,
        10 * length * length,
        (here, grad, weights, weights, shares, queries, keys, values),
    )


def self_back_kernel(
    here_ref, grad_ref, w_out_ref, w_ref, share_ref, q_ref, k_ref, v_ref,
    dqkv_ref, ds_ref, dn_ref, dk_sum, dv_sum,
):
    block = pl.program_id(0)
    here = here_ref[0]
    length, width = q_ref.shape
    count = length // BLOCK
    masks = head_masks(BLOCK, width)

    @pl.when(block == 0)
    def _():
        dk_sum[...] = jnp.zeros_like(dk_sum)
        dv_sum[...] = jnp.zeros_like(dv_sum)

    def one(index):
        def at(quarter):
            return pl.ds(pl.multiple_of(row_place(quarter, here) * BLOCK, BLOCK), BLOCK)

        grad = dot_nn(grad_ref[...], w_out_ref[...]).astype(BF)
        queries = q_ref[at(index), :]
        dq = jnp.zeros((BLOCK, width), F32)
        for head, mask in enumerate(masks):
            own_grad = only(mask, grad)
            own_query = only(mask, queries)
            shares = []
            weighted = []
            for other in range(index + 1):
                lanes = slice(other * BLOCK, (other + 1) * BLOCK)
                low = share_ref[head, :, lanes]
                shares.append(low)
                weighted.append(dot_nt(own_grad, v_ref[at(other), :]) * low.astype(F32))
            inner = weighted[0]
            for part in weighted[1:]:
                inner = inner + part
            inner = jnp.sum(inner, axis=-1, keepdims=True)
            part_q = None
            for other in range(index + 1):
                lanes = slice(other * BLOCK, (other + 1) * BLOCK)
                low = shares[other]
                grad_low = (weighted[other] - low.astype(F32) * inner).astype(BF)
                ds_ref[head, :, lanes] = grad_low
                part = dot_nn(grad_low, k_ref[at(other), :])
                part_q = part if part_q is None else part_q + part
                dk_sum[at(other), :] += dot_tn(grad_low, own_query)
                dv_sum[at(other), :] += dot_tn(low, own_grad)
            dq = dq + only(mask, part_q)
        dqkv_ref[0, at(index), :] = dq.astype(BF)

    for index in range(count):
        pl.when(block == index)(lambda index=index: one(index))

    @pl.when(block == count - 1)
    def _():
        def finish(index, _):
            place = pl.ds(pl.multiple_of(index * BLOCK, BLOCK), BLOCK)
            dk = dk_sum[place, :].astype(BF)
            dv = dv_sum[place, :].astype(BF)
            dqkv_ref[1, place, :] = dk
            dqkv_ref[2, place, :] = dv
            dn_ref[place, :] = (
                dot_nt(dqkv_ref[0, place, :], w_ref[0])
                + dot_nt(dk, w_ref[1])
                + dot_nt(dv, w_ref[2])
            ).astype(BF)
            return 0

        lax.fori_loop(0, count, finish, 0)


def self_backward(here, grad, out_weights, weights, shares, queries, keys, values):
    length, width = grad.shape
    columns = weights.shape[2]
    heads = columns // HEAD_DIM
    blocks = length // BLOCK
    square_spec = pl.BlockSpec((heads, BLOCK, length), lambda i, s: (0, i, 0))
    return call(
        self_back_kernel,
        "self_backward",
        (blocks,),
        [
            pl.BlockSpec((BLOCK, width), lambda i, s: (row_place(i, s[0]), 0)),
            member(0, (width, columns)),
            whole(weights.shape),
            square_spec,
            whole((length, columns)),
            whole((length, columns)),
            whole((length, columns)),
        ],
        [whole((3, length, columns)), square_spec, whole((length, width))],
        [
            jax.ShapeDtypeStruct((3, length, columns), BF),
            jax.ShapeDtypeStruct((heads, length, length), BF),
            jax.ShapeDtypeStruct((length, width), BF),
        ],
        [pltpu.VMEM((length, columns), F32), pltpu.VMEM((length, columns), F32)],
        8 * length * width * columns + 20 * heads * length * length * HEAD_DIM,
        16 * length * length,
        (here, grad, out_weights, weights, shares, queries, keys, values),
    )


def table_kernel(here_ref, low_ref, ds_ref, out_ref):
    block = pl.program_id(0)
    heads = ds_ref.shape[0]
    buckets = out_ref.shape[0] // heads
    group = 4

    @pl.when(block == 0)
    def _():
        out_ref[...] = jnp.zeros_like(out_ref)

    def one_group(number, _):
        first = number * group

        def one_column(column, _):
            lanes = pl.ds(pl.multiple_of(column * 128, 128), 128)
            sums = [[None] * heads for _ in range(group)]
            for strip in range(BLOCK // 16):
                rows = slice(strip * 16, (strip + 1) * 16)
                ids = low_ref[rows, lanes]
                grads = [ds_ref[head, rows, lanes] for head in range(heads)]
                for member_index in range(group):
                    level = (first + member_index).astype(F32).astype(BF)
                    mask = ids == level
                    for head in range(heads):
                        part = jnp.where(mask, grads[head], jnp.zeros_like(grads[head]))
                        held = sums[member_index][head]
                        sums[member_index][head] = part if held is None else held + part
            for member_index in range(group):
                for head in range(heads):
                    summed = sums[member_index][head].astype(F32)
                    place = (first + member_index) * heads + head
                    out_ref[place] += summed[:8] + summed[8:]
            return 0

        lax.fori_loop(0, (block + 1) * (BLOCK // 128), one_column, 0)
        return 0

    lax.fori_loop(0, buckets // group, one_group, 0)


def table_sums(here, low, grads, buckets):
    heads, length, _ = grads.shape
    out = call(
        table_kernel,
        "table_sums",
        (length // BLOCK,),
        [
            pl.BlockSpec((BLOCK, length), lambda i, s: (i, 0)),
            pl.BlockSpec((heads, BLOCK, length), lambda i, s: (0, i, 0)),
        ],
        whole((buckets * heads, 8, 128)),
        jax.ShapeDtypeStruct((buckets * heads, 8, 128), F32),
        [],
        2 * buckets * heads * length * length,
        8 * length * length,
        (here, low, grads),
    )
    return jnp.sum(out, axis=(1, 2)).reshape(buckets, heads)


def local(
    inputs,
    encoder,
    buckets,
    query_weight,
    key_weight,
    value_weight,
    output_weight,
    crossquery,
    crosskey,
    crossvalue,
    crossoutput,
    gate_weight,
    up_weight,
    down_weight,
    norm_gains,
    bias_table,
    cotangent,
):
    here_index = lax.axis_index("tensor")
    here = here_index.astype(jnp.int32).reshape(1)
    head_local = HEADS // lax.axis_size("tensor")
    head_start = here_index * head_local
    gains = norm_gains[0].astype(F32)
    levels = bias_table.shape[0]
    table_local = lax.dynamic_slice_in_dim(bias_table, head_start, head_local, 1)
    table_rows = jnp.zeros((8, 128), F32).at[:head_local, :levels].set(table_local.T.astype(F32))

    residual = inputs.astype(F32)
    rows_self = gather_rows(normalize(residual, gains[0]).astype(BF))
    weights_self = gather_weights(
        jnp.concatenate([query_weight, key_weight, value_weight])
    )
    bias, low_buckets = make_bias(here, buckets, table_rows, head_local)
    weights_cross = gather_weights(
        jnp.stack([output_weight[0].T, crossquery[0], crosskey[0], crossvalue[0], crossoutput[0].T])
    )
    memory_all = gather_rows(encoder)
    weights_ff = gather_weights(jnp.stack([gate_weight[0], up_weight[0], down_weight[0].T]))
    grad_out_all = gather_rows(cotangent)

    queries, keys, values, shares, mixture = self_forward(here, rows_self, weights_self, bias)
    middle = residual + scatter_sums(dot_nt(mixture, weights_cross[0]).astype(BF))

    cross_keys = dot_nn(memory_all, weights_cross[2]).astype(BF)
    cross_values = dot_nn(memory_all, weights_cross[3]).astype(BF)
    rows_cross = gather_rows(normalize(middle, gains[1]).astype(BF))
    cross_queries, cross_shares, cross_mixture = cross_forward(
        here, rows_cross, weights_cross, cross_keys, cross_values
    )
    late = middle + scatter_sums(dot_nt(cross_mixture, weights_cross[4]).astype(BF))

    grad_hidden = dot_nn(grad_out_all, weights_ff[2])
    rows_ff = gather_rows(normalize(late, gains[2]).astype(BF))
    hidden, grad_gate, grad_up, dn_ff = feed_forward(here, rows_ff, weights_ff, grad_hidden)
    dn = scatter_sums(dn_ff)
    grad_flow = cotangent.astype(F32)
    back, gain_ff = normalize_back(late, gains[2], dn)
    grad_flow = grad_flow + back
    outputs = (late + scatter_sums(dot_nt(hidden, weights_ff[2]).astype(BF))).astype(BF)
    grads_ff = reduce_weights(
        jnp.stack([dot_tn(rows_ff, grad_gate), dot_tn(rows_ff, grad_up), dot_tn(grad_out_all, hidden)]).astype(BF)
    )

    grad_late = gather_rows(grad_flow.astype(BF))
    cross_dq, cross_dkv, dn_cross = cross_backward(
        here, grad_late, weights_cross, cross_shares, cross_queries, cross_keys, cross_values
    )
    dn = scatter_sums(dn_cross)
    back, gain_cross = normalize_back(middle, gains[1], dn)
    grad_flow = grad_flow + back
    grad_encoder = scatter_sums(
        (dot_nt(cross_dkv[0], weights_cross[2]) + dot_nt(cross_dkv[1], weights_cross[3])).astype(BF)
    )
    grads_cross = reduce_weights(
        jnp.stack(
            [
                dot_tn(rows_cross, cross_dq),
                dot_tn(memory_all, cross_dkv[0]),
                dot_tn(memory_all, cross_dkv[1]),
                dot_tn(grad_late, cross_mixture),
            ]
        ).astype(BF)
    )

    grad_middle = gather_rows(grad_flow.astype(BF))
    dqkv, ds, dn_self = self_backward(
        here, grad_middle, weights_cross, weights_self, shares, queries, keys, values
    )
    dn = scatter_sums(dn_self)
    back, gain_self = normalize_back(residual, gains[0], dn)
    grad_flow = grad_flow + back
    grads_self = reduce_weights(
        jnp.stack(
            [
                dot_tn(rows_self, dqkv[0]),
                dot_tn(rows_self, dqkv[1]),
                dot_tn(rows_self, dqkv[2]),
                dot_tn(grad_middle, mixture),
            ]
        ).astype(BF)
    )

    table_part = table_sums(here, low_buckets, ds, levels)
    table_full = lax.dynamic_update_slice_in_dim(
        jnp.zeros(bias_table.shape, F32), table_part, head_start, 1
    )
    small = jnp.concatenate(
        [jnp.stack([gain_self, gain_cross, gain_ff]).reshape(-1), table_full.reshape(-1)]
    ).reshape(-1, 128)
    small = sum_everywhere(small).reshape(-1)
    gain_size = norm_gains.size
    gain_sums = small[:gain_size].reshape(norm_gains.shape)
    table_full = small[gain_size:].reshape(bias_table.shape)

    return (
        outputs,
        grad_flow,
        grad_encoder,
        grads_self[0:1],
        grads_self[1:2],
        grads_self[2:3],
        grads_self[3].T[None],
        grads_cross[0:1],
        grads_cross[1:2],
        grads_cross[2:3],
        grads_cross[3].T[None],
        grads_ff[0:1],
        grads_ff[1:2],
        grads_ff[2].T[None],
        gain_sums,
        table_full,
    )


def solution(mesh):
    rows = P(("dp", "tensor"), None)
    column = P(None, "dp", "tensor")
    row = P(None, "tensor", "dp")
    weights = (column, column, column, row, column, column, column, row, column, column, row)
    in_specs = (rows, rows, P()) + weights + (P(), P(), rows)
    out_specs = (rows, rows, rows) + weights + (P(), P())
    return jax.shard_map(local, mesh=mesh, in_specs=in_specs, out_specs=out_specs, check_vma=False)
```

```python
import jax
import jax.numpy as jnp
from jax import lax
from jax.experimental import pallas as pl
from jax.experimental.pallas import tpu as pltpu
from jax.sharding import PartitionSpec as P

HEADS = 12
HEAD_DIM = 64
EPS = 1e-06
BF = jnp.bfloat16
F32 = jnp.float32
BLOCK = 256
VMEM_LIMIT = 40 * 1024 * 1024
VMEM_MOST = 60 * 1024 * 1024
FLOP_PER_US = 1.15e9
EXPECTED_US = {
    "pack_self": 1.6,
    "pack_cross": 1.6,
    "pack_ff": 1.8,
    "position_bias": 8,
    "self_forward": 10,
    "cross_projections": 1.6,
    "cross_forward": 7,
    "feed_forward": 7,
    "down_projection": 2,
    "cross_backward": 10,
    "grads_ff": 4,
    "grads_cross": 4,
    "memory_grads": 1,
    "self_backward": 14,
    "grads_self": 3.5,
    "table_sums": 14,
}

CORE = [(0, 1), (1, 0), (2, 3), (3, 2)]
CHIP = [(0, 2), (2, 0), (1, 3), (3, 1)]
SEND_FIRST = (2, 3, 0, 1)


def after(value, *others):
    return lax.optimization_barrier((value,) + others)[0]


def gather_rows(piece, meanwhile=None):
    far = lax.ppermute(piece, "tensor", CHIP)
    near = lax.ppermute(piece, "tensor", CORE)
    if meanwhile is not None:
        far = after(far, *meanwhile(piece))
    last = lax.ppermute(far, "tensor", CORE)
    return (piece, far, near, last)


def start_sums(send, keep):
    rows = keep.shape[0] // 2
    near = lax.ppermute(send, "tensor", CORE)
    outgoing = (keep[rows:].astype(F32) + near[rows:].astype(F32)).astype(BF)
    return (keep, near), outgoing


def finish_sums(first, outgoing, *meanwhile):
    keep, near = first
    rows = outgoing.shape[0]
    far = lax.ppermute(outgoing, "tensor", CHIP)
    if meanwhile:
        far = after(far, *meanwhile)
    return keep[:rows].astype(F32) + near[:rows].astype(F32) + far.astype(F32)


def swap_pairs(size, bit):
    return [(i, i ^ bit) for i in range(size)]


class Gathering:

    def __init__(self, shard):
        self.held = [shard]
        self.axis = 1
        self.bit = lax.axis_size("dp") // 2

    def step(self, *waits, part=None, split=False):
        size = lax.axis_size("dp")
        second = (lax.axis_index("dp") & self.bit) != 0
        parts = []
        for number, held in enumerate(self.held):
            if part is not None and number != part:
                parts.append(held)
                continue
            other = lax.ppermute(held, "dp", swap_pairs(size, self.bit))
            if waits:
                other = after(other, *waits)
            for low in range(held.shape[0] if split else 1):
                pick = slice(low, low + 1) if split else slice(None)
                mine, theirs = held[pick], other[pick]
                parts.append(
                    jnp.stack(
                        [jnp.where(second, theirs, mine), jnp.where(second, mine, theirs)],
                        axis=self.axis,
                    )
                )
        self.held = parts
        if part is None or part == len(parts) - 1:
            self.axis += 1
            self.bit //= 2

    def finish(self):
        while self.bit >= 1:
            self.step()
        return [held.reshape(held.shape[0], -1, held.shape[-1]) for held in self.held]


class Reduction:

    def __init__(self, send, keep):
        self.send, self.keep = send, keep
        self.bit = 1
        self.shape = keep.shape

    def step(self, *waits):
        size = lax.axis_size("dp")
        me = lax.axis_index("dp")
        received = lax.ppermute(self.send, "dp", swap_pairs(size, self.bit))
        if waits:
            received = after(received, *waits)
        current = self.keep.astype(F32) + received.astype(F32)
        self.bit *= 2
        count, _, rows, columns = self.shape
        self.send = self.keep = None
        if self.bit >= size:
            self.total = current.reshape(count, rows, columns)
            return
        current = current.reshape(count, size // (2 * self.bit), 2, rows, columns)
        mine = jnp.where((me & self.bit) != 0, 1, 0)
        self.send = lax.dynamic_index_in_dim(current, 1 - mine, 2, keepdims=False).astype(BF)
        self.keep = lax.dynamic_index_in_dim(current, mine, 2, keepdims=False)

    @staticmethod
    def joined(parts):
        whole_sum = Reduction(
            jnp.concatenate([part.send for part in parts]),
            jnp.concatenate([part.keep for part in parts]),
        )
        whole_sum.bit = parts[0].bit
        whole_sum.shape = (sum(part.shape[0] for part in parts),) + parts[0].shape[1:]
        return whole_sum

    def finish(self, *waits):
        while self.send is not None:
            self.step(*waits)
        return self.total


def sum_everywhere(values, meanwhile):
    for pairs in (CORE, CHIP):
        values = values + lax.ppermute(values, "tensor", pairs)
    values = after(values, meanwhile)
    size = lax.axis_size("dp")
    bit = 1
    while bit < size:
        values = values + lax.ppermute(values, "dp", swap_pairs(size, bit))
        bit *= 2
    return values


def dot_nn(left, right):
    return jnp.dot(left, right, preferred_element_type=F32)


def dot_nt(left, right):
    return lax.dot_general(left, right, (((1,), (1,)), ((), ())), preferred_element_type=F32)


def dot_tn(left, right):
    return lax.dot_general(left, right, (((0,), (0,)), ((), ())), preferred_element_type=F32)


def normalize(values, gain_row):
    inverse_root = lax.rsqrt(jnp.mean(values * values, axis=-1, keepdims=True) + EPS)
    return values * inverse_root * gain_row


def normalize_back(values, gain_row, grad):
    inverse_root = lax.rsqrt(jnp.mean(values * values, axis=-1, keepdims=True) + EPS)
    scaled = values * inverse_root
    gain_grad = jnp.sum(grad * scaled, axis=0)
    inner = grad * gain_row
    back = inverse_root * (inner - scaled * jnp.mean(inner * scaled, axis=-1, keepdims=True))
    return back, gain_grad


def row_place(block, here):
    turned = lax.bitwise_xor(block, here)
    return lax.bitwise_or(
        lax.shift_left(lax.bitwise_and(turned, 1), 1), lax.shift_right_logical(turned, 1)
    )


def head_masks(rows, columns):
    lane_head = lax.broadcasted_iota(jnp.int32, (rows, columns), 1) // HEAD_DIM
    return [lane_head == head for head in range(columns // HEAD_DIM)]


def only(mask, values):
    return jnp.where(mask, values, jnp.zeros_like(values))


def call(kernel, name, grid, in_specs, out_specs, out_shape, scratch, flops, moved, args, tokens=(), limit=VMEM_LIMIT):
    inputs = 1 + len(in_specs)

    def run(*refs):
        kernel(*refs[:inputs], *refs[inputs + len(tokens) :])

    return pl.pallas_call(
        run,
        grid_spec=pltpu.PrefetchScalarGridSpec(
            num_scalar_prefetch=1,
            grid=grid,
            in_specs=list(in_specs) + [pl.BlockSpec(memory_space=pl.ANY)] * len(tokens),
            out_specs=out_specs,
            scratch_shapes=scratch,
        ),
        out_shape=out_shape,
        compiler_params=pltpu.CompilerParams(
            dimension_semantics=("arbitrary",) * len(grid), vmem_limit_bytes=limit
        ),
        cost_estimate=pl.CostEstimate(
            flops=int(EXPECTED_US[name] * FLOP_PER_US), bytes_accessed=1, transcendentals=0
        ),
        name=name,
    )(*args, *tokens)


def whole(shape):
    return pl.BlockSpec(shape, lambda i, s: (0,) * len(shape))


def member(index, shape):
    return pl.BlockSpec((None,) + shape, lambda i, s: (index,) + (0,) * len(shape))


def turn(step):
    return lax.rem(step + 2, 4)


def quarter_spec(columns):
    return pl.BlockSpec((BLOCK, columns), lambda i, s: (turn(i), 0))


def piece_specs(pieces):
    return [whole(piece.shape) for piece in pieces]


def half_specs(width):
    return [
        pl.BlockSpec((BLOCK, width), lambda i, s: (jnp.minimum(i, 1), 0)),
        pl.BlockSpec((BLOCK, width), lambda i, s: (jnp.maximum(i - 2, 0), 0)),
    ]


def half_shapes(width):
    return [jax.ShapeDtypeStruct((2 * BLOCK, width), BF)] * 2


def store_half(step, send_ref, keep_ref, values):
    @pl.when(step < 2)
    def _():
        send_ref[...] = values

    @pl.when(step >= 2)
    def _():
        keep_ref[...] = values


def take_quarter(step, refs, target):
    for number, quarter in enumerate(SEND_FIRST):

        @pl.when(step == number)
        def _(quarter=quarter):
            target[...] = refs[quarter][...]


def pack_kernel(here_ref, *refs):
    packed_ref = refs[-1]
    columns = refs[0].shape[2]
    for number, ref in enumerate(refs[:-1]):
        values = ref[0] if number < len(refs) - 2 else ref[0].T
        if len(packed_ref.shape) == 3:
            packed_ref[number] = values
        else:
            packed_ref[:, number * columns : (number + 1) * columns] = values


def pack(here, name, matrices, flat=False):
    rows, columns = matrices[0].shape[1:]
    shape = (rows, len(matrices) * columns) if flat else (len(matrices), rows, columns)
    if rows % 16:
        turned = list(matrices[:-1]) + [matrices[-1].transpose(0, 2, 1)]
        return jnp.concatenate(turned, axis=2)[0] if flat else jnp.concatenate(turned)
    return call(
        pack_kernel,
        name,
        (1,),
        [whole(matrix.shape) for matrix in matrices],
        whole(shape),
        jax.ShapeDtypeStruct(shape, BF),
        [],
        0,
        0,
        (here, *matrices),
        limit=VMEM_MOST,
    )


def bias_kernel(here_ref, buckets_ref, table_ref, bias_ref):
    block = pl.program_id(0)
    heads = bias_ref.shape[0]
    length = buckets_ref.shape[1]
    for column in range(length // 128):

        @pl.when(column * 128 < (block + 1) * BLOCK)
        def _():
            lanes = slice(column * 128, (column + 1) * 128)
            ids = buckets_ref[:, lanes]
            for head in range(heads):
                row = jnp.broadcast_to(table_ref[head : head + 1, :], ids.shape)
                picked = jnp.take_along_axis(row, ids, axis=1, mode="promise_in_bounds")
                bias_ref[head, :, lanes] = picked.astype(BF)


def make_bias(here, buckets, table_rows, heads):
    length = buckets.shape[0]
    blocks = length // BLOCK
    return call(
        bias_kernel,
        "position_bias",
        (blocks,),
        [pl.BlockSpec((BLOCK, length), lambda i, s: (i, 0)), whole(table_rows.shape)],
        pl.BlockSpec((heads, BLOCK, length), lambda i, s: (0, i, 0)),
        jax.ShapeDtypeStruct((heads, length, length), BF),
        [],
        0,
        12 * length * length,
        (here, buckets, table_rows),
        limit=VMEM_MOST,
    )


def self_kernel(
    here_ref, *refs
):
    pieces = refs[:4]
    w_ref, bias_ref, q_ref, k_ref, v_ref, share_ref, mix_ref, send_ref, keep_ref = refs[4:]
    block = pl.program_id(0)
    here = here_ref[0]
    length, width = q_ref.shape
    masks = head_masks(BLOCK, width)

    @pl.when(block == 0)
    def _():
        for quarter, piece in enumerate(pieces):
            rows = piece[...]
            place = slice(quarter * BLOCK, (quarter + 1) * BLOCK)
            for number, target in enumerate((q_ref, k_ref, v_ref)):
                target[place, :] = dot_nn(rows, w_ref[number]).astype(BF)

    def one(index):
        def at(quarter):
            return pl.ds(pl.multiple_of(row_place(quarter, here) * BLOCK, BLOCK), BLOCK)

        queries = q_ref[at(index), :]
        keys = [k_ref[at(other), :] for other in range(index + 1)]
        values = [v_ref[at(other), :] for other in range(index + 1)]
        visible = lax.broadcasted_iota(jnp.int32, (BLOCK, BLOCK), 1) <= lax.broadcasted_iota(
            jnp.int32, (BLOCK, BLOCK), 0
        )
        mixture = jnp.zeros((BLOCK, width), F32)
        for head, mask in enumerate(masks):
            own = only(mask, queries)
            scores = []
            for other in range(index + 1):
                lanes = slice(other * BLOCK, (other + 1) * BLOCK)
                score = dot_nt(own, keys[other]) + bias_ref[head, :, lanes].astype(F32)
                if other == index:
                    score = jnp.where(visible, score, -1000000000.0)
                scores.append(score)
            highest = scores[0]
            for score in scores[1:]:
                highest = jnp.maximum(highest, score)
            highest = jnp.max(highest, axis=-1, keepdims=True)
            raised = [jnp.exp(score - highest) for score in scores]
            total = raised[0]
            for part in raised[1:]:
                total = total + part
            inverse = 1.0 / jnp.sum(total, axis=-1, keepdims=True)
            mixed = None
            for other in range(index + 1):
                lanes = slice(other * BLOCK, (other + 1) * BLOCK)
                share = (raised[other] * inverse).astype(BF)
                share_ref[head, :, lanes] = share
                part = dot_nn(share, values[other])
                mixed = part if mixed is None else mixed + part
            mixture = mixture + only(mask, mixed)
        mix_ref[at(index), :] = mixture.astype(BF)

    for index in range(length // BLOCK):
        pl.when(block == index)(lambda index=index: one(index))

    @pl.when(block == length // BLOCK - 1)
    def _():
        half = length // 2
        for quarter in range(2):
            place = slice(quarter * BLOCK, (quarter + 1) * BLOCK)
            away = slice(half + quarter * BLOCK, half + (quarter + 1) * BLOCK)
            send_ref[place, :] = dot_nt(mix_ref[away, :], w_ref[3]).astype(BF)
            keep_ref[place, :] = dot_nt(mix_ref[place, :], w_ref[3]).astype(BF)


def self_forward(here, pieces, weights, bias, tokens):
    heads, length, _ = bias.shape
    width, columns = weights.shape[1:]
    blocks = length // BLOCK
    whole_rows = jax.ShapeDtypeStruct((length, columns), BF)
    square_spec = pl.BlockSpec((heads, BLOCK, length), lambda i, s: (0, i, 0))
    return call(
        self_kernel,
        "self_forward",
        (blocks,),
        piece_specs(pieces) + [whole(weights.shape), square_spec],
        [whole((length, columns))] * 3
        + [square_spec, whole((length, columns))]
        + [whole((length // 2, width))] * 2,
        [whole_rows] * 3
        + [jax.ShapeDtypeStruct((heads, length, length), BF), whole_rows]
        + half_shapes(width),
        [],
        2 * length * width * columns * 4 + 16 * heads * length * length * HEAD_DIM,
        16 * length * length,
        (here, *pieces, weights, bias),
        tokens,
    )


def cross_keys_kernel(here_ref, *refs):
    pieces = refs[:4]
    wk_ref, wv_ref, k_ref, v_ref = refs[4:]
    rows = pieces[0].shape[0]
    for quarter, piece in enumerate(pieces):
        place = slice(quarter * rows, (quarter + 1) * rows)
        values = piece[...]
        k_ref[place, :] = dot_nn(values, wk_ref[...]).astype(BF)
        v_ref[place, :] = dot_nn(values, wv_ref[...]).astype(BF)


def cross_projections(here, pieces, weights, tokens):
    rows, width = pieces[0].shape
    columns = weights.shape[2]
    shape = (4 * rows, columns)
    return call(
        cross_keys_kernel,
        "cross_projections",
        (1,),
        piece_specs(pieces) + [member(1, (width, columns)), member(2, (width, columns))],
        [whole(shape)] * 2,
        [jax.ShapeDtypeStruct(shape, BF)] * 2,
        [],
        16 * rows * width * columns,
        16 * rows * width,
        (here, *pieces, weights, weights),
        tokens,
    )


def cross_kernel(here_ref, *refs):
    pieces = refs[:4]
    w_ref, wo_ref, k_ref, v_ref, q_ref, share_ref, mix_ref, send_ref, keep_ref, rows_ref = refs[4:]
    step = pl.program_id(0)
    width = q_ref.shape[1]
    masks = head_masks(BLOCK, width)
    take_quarter(step, pieces, rows_ref)
    queries = dot_nn(rows_ref[...], w_ref[...]).astype(BF)
    q_ref[...] = queries
    keys = k_ref[...]
    values = v_ref[...]
    mixture = jnp.zeros((BLOCK, width), F32)
    for head, mask in enumerate(masks):
        scores = dot_nt(only(mask, queries), keys)
        raised = jnp.exp(scores - jnp.max(scores, axis=-1, keepdims=True))
        share = (raised * (1.0 / jnp.sum(raised, axis=-1, keepdims=True))).astype(BF)
        share_ref[head] = share
        mixture = mixture + only(mask, dot_nn(share, values))
    mixture = mixture.astype(BF)
    mix_ref[...] = mixture
    store_half(step, send_ref, keep_ref, dot_nt(mixture, wo_ref[...]).astype(BF))


def cross_forward(here, pieces, weights, keys, values, tokens):
    width, columns = weights.shape[1:]
    length = 4 * BLOCK
    heads = columns // HEAD_DIM
    sources = keys.shape[0]
    whole_rows = jax.ShapeDtypeStruct((length, columns), BF)
    row_spec = quarter_spec(columns)
    return call(
        cross_kernel,
        "cross_forward",
        (4,),
        piece_specs(pieces)
        + [
            member(0, (width, columns)),
            member(3, (width, columns)),
            whole((sources, columns)),
            whole((sources, columns)),
        ],
        [row_spec, pl.BlockSpec((heads, BLOCK, sources), lambda i, s: (0, turn(i), 0)), row_spec]
        + half_specs(width),
        [whole_rows, jax.ShapeDtypeStruct((heads, length, sources), BF), whole_rows]
        + half_shapes(width),
        [pltpu.VMEM((BLOCK, width), BF)],
        4 * length * width * columns + 16 * heads * length * sources * HEAD_DIM,
        8 * length * length,
        (here, *pieces, weights, weights, keys, values),
        tokens,
    )


def ff_kernel(here_ref, *refs):
    pieces = refs[:4]
    grads = refs[4:8]
    w_gate_ref, w_up_ref, w_down_ref = refs[8:11]
    hidden_ref, grad_gate_ref, grad_up_ref, send_ref, keep_ref, rows_ref, back_ref = refs[11:]
    step = pl.program_id(0)
    take_quarter(step, pieces, rows_ref)
    take_quarter(step, grads, back_ref)
    rows = rows_ref[...]
    gate = dot_nn(rows, w_gate_ref[0])
    up = dot_nn(rows, w_up_ref[0])
    grad = dot_nn(back_ref[...], w_down_ref[0])
    slope = 0.7978845608028654
    square = gate * gate
    bent = jnp.tanh(slope * (gate + 0.044715 * (square * gate)))
    half = 0.5 * (1.0 + bent)
    active = gate * half
    change = half + 0.5 * gate * (1.0 - bent * bent) * slope * (1.0 + 3.0 * 0.044715 * square)
    hidden_ref[...] = (active * up).astype(BF)
    grad_gate = (grad * up * change).astype(BF)
    grad_up = (grad * active).astype(BF)
    grad_gate_ref[...] = grad_gate
    grad_up_ref[...] = grad_up
    dn = dot_nt(grad_gate, w_gate_ref[0]) + dot_nt(grad_up, w_up_ref[0])
    store_half(step, send_ref, keep_ref, dn.astype(BF))


def feed_forward(here, pieces, grads, weights):
    width, columns = weights[0].shape[1:]
    length = 4 * BLOCK
    row_spec = quarter_spec(columns)
    whole_rows = jax.ShapeDtypeStruct((length, columns), BF)
    return call(
        ff_kernel,
        "feed_forward",
        (4,),
        piece_specs(pieces) + piece_specs(grads) + piece_specs(weights),
        [row_spec] * 3 + half_specs(width),
        [whole_rows] * 3 + half_shapes(width),
        [pltpu.VMEM((BLOCK, width), BF), pltpu.VMEM((BLOCK, width), BF)],
        10 * length * width * columns,
        12 * length * width,
        (here, *pieces, *grads, *weights),
    )


def down_kernel(here_ref, hidden_ref, w_ref, send_ref, keep_ref):
    step = pl.program_id(0)
    store_half(step, send_ref, keep_ref, dot_nt(hidden_ref[...], w_ref[...]).astype(BF))


def down_projection(here, hidden, weights, tokens):
    width, columns = weights.shape[1:]
    length = 4 * BLOCK
    return call(
        down_kernel,
        "down_projection",
        (4,),
        [quarter_spec(columns), member(0, (width, columns))],
        half_specs(width),
        half_shapes(width),
        [],
        2 * length * width * columns,
        6 * length * width,
        (here, hidden, weights),
        tokens,
    )


def weight_grads_kernel(plan, split, bit_ref, *refs):
    pieces = max(first for first, _ in plan) + 4
    grads = max(number for _, number in plan) + 1
    piece_refs, refs = refs[:pieces], refs[pieces:]
    grad_refs, refs = refs[:grads], refs[grads:]
    bit = bit_ref[0]
    turned = {}
    for slot, (first, number) in enumerate(plan):
        if first not in turned:
            turned = {first: [piece_refs[first + part][...].T for part in range(4)]}
        grad_ref = grad_refs[number]
        rows = turned[first][0].shape[1]
        summed = None
        for part in range(4):
            place = slice(part * rows, (part + 1) * rows)
            addend = dot_nn(turned[first][part], grad_ref[place, :])
            summed = addend if summed is None else summed + addend
        if not split:
            start = sum(grad_refs[earlier].shape[1] for _, earlier in plan[:slot])
            refs[0][:, start : start + grad_ref.shape[1]] = summed.astype(BF)
            continue
        send_ref, keep_ref, sum_ref = refs
        sum_ref[...] = summed
        half, block = send_ref.shape[1:3]
        for number_here in range(half):
            for target, side in ((send_ref, 1 - bit), (keep_ref, bit)):
                start = pl.multiple_of((2 * number_here + side) * block, block)
                target[slot, number_here] = sum_ref[pl.ds(start, block), :].astype(BF)


def weight_grads(name, groups, tokens=(), flat=False):
    size = lax.axis_size("dp")
    bit = lax.bitwise_and(lax.axis_index("dp").astype(jnp.int32), 1)
    plan = []
    pieces = []
    grads = []
    for group, arrays in groups:
        for array in arrays:
            plan.append((len(pieces), len(grads)))
            grads.append(array)
        pieces.extend(group)
    width = pieces[0].shape[1]
    columns = grads[0].shape[1]
    block = width // size
    split = block % 16 == 0 and not flat
    if split:
        shapes = [(len(plan), size // 2, block, columns)] * 2
    else:
        shapes = [(width, sum(grad.shape[1] for grad in grads))]
    out = call(
        lambda *refs: weight_grads_kernel(tuple(plan), split, *refs),
        name,
        (1,),
        [whole(piece.shape) for piece in pieces] + [whole(grad.shape) for grad in grads],
        [whole(shape) for shape in shapes],
        [jax.ShapeDtypeStruct(shape, BF) for shape in shapes],
        [pltpu.VMEM((width, columns), F32)] if split else [],
        sum(2 * grad.shape[0] * width * columns for grad in grads),
        4 * len(plan) * width * columns,
        (bit.reshape(1), *pieces, *grads),
        tokens,
        VMEM_MOST if name == "grads_ff" else VMEM_LIMIT,
    )
    if split:
        return out
    if flat:
        return out[0]
    halves = out[0].reshape(size // 2, 2, block, len(plan), columns).transpose(3, 0, 1, 2, 4)
    return [
        lax.dynamic_index_in_dim(halves, side, 2, keepdims=False) for side in (1 - bit, bit)
    ]


def cross_back_kernel(here_ref, *refs):
    pieces = refs[:4]
    w_out_ref, w_q_ref, share_ref, q_ref, k_ref, v_ref = refs[4:10]
    dq_ref, dk_ref, dv_ref, send_ref, keep_ref, dk_sum, dv_sum, rows_ref = refs[10:]
    step = pl.program_id(0)
    width = q_ref.shape[1]
    masks = head_masks(BLOCK, width)
    take_quarter(step, pieces, rows_ref)
    grad = dot_nn(rows_ref[...], w_out_ref[...]).astype(BF)
    queries = q_ref[...]
    keys = k_ref[...]
    values = v_ref[...]

    @pl.when(step == 0)
    def _():
        dk_sum[...] = jnp.zeros_like(dk_sum)
        dv_sum[...] = jnp.zeros_like(dv_sum)

    dq = jnp.zeros((BLOCK, width), F32)
    dk = dk_sum[...]
    dv = dv_sum[...]
    for head, mask in enumerate(masks):
        own_grad = only(mask, grad)
        low = share_ref[head]
        share = low.astype(F32)
        weighted = dot_nt(own_grad, values) * share
        inner = jnp.sum(weighted, axis=-1, keepdims=True)
        grad_low = (weighted - share * inner).astype(BF)
        dq = dq + only(mask, dot_nn(grad_low, keys))
        dk = dk + dot_tn(grad_low, only(mask, queries))
        dv = dv + dot_tn(low, own_grad)
    dk_sum[...] = dk
    dv_sum[...] = dv
    dq = dq.astype(BF)
    dq_ref[...] = dq
    store_half(step, send_ref, keep_ref, dot_nt(dq, w_q_ref[...]).astype(BF))

    @pl.when(step == pl.num_programs(0) - 1)
    def _():
        dk_ref[...] = dk.astype(BF)
        dv_ref[...] = dv.astype(BF)


def cross_backward(here, pieces, weights, shares, queries, keys, values):
    width, columns = weights.shape[1:]
    length = 4 * BLOCK
    heads = columns // HEAD_DIM
    sources = keys.shape[0]
    row_spec = quarter_spec(columns)
    source_spec = whole((sources, columns))
    source_shape = jax.ShapeDtypeStruct((sources, columns), BF)
    return call(
        cross_back_kernel,
        "cross_backward",
        (4,),
        piece_specs(pieces)
        + [
            member(3, (width, columns)),
            member(0, (width, columns)),
            pl.BlockSpec((heads, BLOCK, sources), lambda i, s: (0, turn(i), 0)),
            row_spec,
            source_spec,
            source_spec,
        ],
        [row_spec, source_spec, source_spec] + half_specs(width),
        [jax.ShapeDtypeStruct((length, columns), BF), source_shape, source_shape]
        + half_shapes(width),
        [
            pltpu.VMEM((sources, columns), F32),
            pltpu.VMEM((sources, columns), F32),
            pltpu.VMEM((BLOCK, width), BF),
        ],
        4 * length * width * columns + 32 * heads * length * sources * HEAD_DIM,
        10 * length * length,
        (here, *pieces, weights, weights, shares, queries, keys, values),
    )


def memory_kernel(here_ref, dk_ref, dv_ref, wk_ref, wv_ref, send_ref, keep_ref):
    half = send_ref.shape[0]
    for target, start in ((send_ref, half), (keep_ref, 0)):
        place = slice(start, start + half)
        summed = dot_nt(dk_ref[place, :], wk_ref[...]) + dot_nt(dv_ref[place, :], wv_ref[...])
        target[...] = summed.astype(BF)


def memory_grads(here, dk, dv, weights, tokens):
    width, columns = weights.shape[1:]
    sources = dk.shape[0]
    half = (sources // 2, width)
    return call(
        memory_kernel,
        "memory_grads",
        (1,),
        [whole(dk.shape)] * 2 + [member(1, (width, columns)), member(2, (width, columns))],
        [whole(half)] * 2,
        [jax.ShapeDtypeStruct(half, BF)] * 2,
        [],
        4 * sources * width * columns,
        4 * sources * width,
        (here, dk, dv, weights, weights),
        tokens,
    )


def self_back_kernel(here_ref, *refs):
    pieces = refs[:4]
    w_ref, share_ref, q_ref, k_ref, v_ref = refs[4:9]
    dq_ref, dk_ref, dv_ref, ds_ref, send_ref, keep_ref, dk_sum, dv_sum, grad_all = refs[9:]
    block = pl.program_id(0)
    here = here_ref[0]
    length, width = q_ref.shape
    count = length // BLOCK
    masks = head_masks(BLOCK, width)

    @pl.when(block == 0)
    def _():
        dk_sum[...] = jnp.zeros_like(dk_sum)
        dv_sum[...] = jnp.zeros_like(dv_sum)
        for quarter, piece in enumerate(pieces):
            place = slice(quarter * BLOCK, (quarter + 1) * BLOCK)
            grad_all[place, :] = dot_nn(piece[...], w_ref[3]).astype(BF)

    def one(index):
        def at(quarter):
            return pl.ds(pl.multiple_of(row_place(quarter, here) * BLOCK, BLOCK), BLOCK)

        grad = grad_all[at(index), :]
        queries = q_ref[at(index), :]
        dq = jnp.zeros((BLOCK, width), F32)
        for head, mask in enumerate(masks):
            own_grad = only(mask, grad)
            own_query = only(mask, queries)
            shares = []
            weighted = []
            for other in range(index + 1):
                lanes = slice(other * BLOCK, (other + 1) * BLOCK)
                low = share_ref[head, :, lanes]
                shares.append(low)
                weighted.append(dot_nt(own_grad, v_ref[at(other), :]) * low.astype(F32))
            inner = weighted[0]
            for part in weighted[1:]:
                inner = inner + part
            inner = jnp.sum(inner, axis=-1, keepdims=True)
            part_q = None
            for other in range(index + 1):
                lanes = slice(other * BLOCK, (other + 1) * BLOCK)
                low = shares[other]
                grad_low = (weighted[other] - low.astype(F32) * inner).astype(BF)
                ds_ref[head, :, lanes] = grad_low
                part = dot_nn(grad_low, k_ref[at(other), :])
                part_q = part if part_q is None else part_q + part
                dk_sum[at(other), :] += dot_tn(grad_low, own_query)
                dv_sum[at(other), :] += dot_tn(low, own_grad)
            dq = dq + only(mask, part_q)
        dq_ref[at(index), :] = dq.astype(BF)

    for index in range(count):
        pl.when(block == index)(lambda index=index: one(index))

    @pl.when(block == count - 1)
    def _():
        for quarter in range(count):
            place = slice(quarter * BLOCK, (quarter + 1) * BLOCK)
            dk = dk_sum[place, :].astype(BF)
            dv = dv_sum[place, :].astype(BF)
            dk_ref[place, :] = dk
            dv_ref[place, :] = dv
            dn = dot_nt(dq_ref[place, :], w_ref[0]) + dot_nt(dk, w_ref[1]) + dot_nt(dv, w_ref[2])
            target = keep_ref if quarter < 2 else send_ref
            target[slice(quarter % 2 * BLOCK, (quarter % 2 + 1) * BLOCK), :] = dn.astype(BF)


def self_backward(here, pieces, weights, shares, queries, keys, values, tokens):
    heads, length, _ = shares.shape
    width, columns = weights.shape[1:]
    blocks = length // BLOCK
    square_spec = pl.BlockSpec((heads, BLOCK, length), lambda i, s: (0, i, 0))
    rows = whole((length, columns))
    return call(
        self_back_kernel,
        "self_backward",
        (blocks,),
        piece_specs(pieces) + [whole(weights.shape), square_spec, rows, rows, rows],
        [rows, rows, rows, square_spec] + [whole((length // 2, width))] * 2,
        [jax.ShapeDtypeStruct((length, columns), BF)] * 3
        + [jax.ShapeDtypeStruct((heads, length, length), BF)]
        + half_shapes(width),
        [
            pltpu.VMEM((length, columns), F32),
            pltpu.VMEM((length, columns), F32),
            pltpu.VMEM((length, columns), BF),
        ],
        8 * length * width * columns + 20 * heads * length * length * HEAD_DIM,
        16 * length * length,
        (here, *pieces, weights, shares, queries, keys, values),
        tokens,
    )


def table_kernel(first, here_ref, buckets_ref, ds_ref, out_ref):
    step = pl.program_id(0)
    heads = ds_ref.shape[0]
    group = 16
    levels = out_ref.shape[0] // group

    @pl.when(step == 0)
    def _():
        out_ref[...] = jnp.zeros_like(out_ref)

    def one(index):
        keys = (index + 1) * BLOCK
        level_ids = lax.broadcasted_iota(jnp.int32, (group, levels, BLOCK), 1)

        def strip(number, _):
            rows = pl.ds(pl.multiple_of(number * group, group), group)
            total = None
            for start in range(0, keys, BLOCK):
                lanes = slice(start, start + BLOCK)
                ids = buckets_ref[rows, lanes]
                chosen = jnp.where(ids[:, None, :] == level_ids, 1.0, 0.0).astype(BF)
                grads = ds_ref[:, rows, lanes].reshape(heads * group, BLOCK)
                part = dot_nt(chosen.reshape(group * levels, BLOCK), grads)
                total = part if total is None else total + part
            out_ref[...] += total
            return 0

        lax.fori_loop(0, BLOCK // group, strip, 0)

    for index in range(ds_ref.shape[2] // BLOCK):
        pl.when(step + first == index)(lambda index=index: one(index))


def table_sums(here, buckets, grads, levels, first, count, tokens):
    heads, length, _ = grads.shape
    return call(
        lambda *refs: table_kernel(first, *refs),
        "table_sums",
        (count,),
        [
            pl.BlockSpec((BLOCK, length), lambda i, s: (i + first, 0)),
            pl.BlockSpec((heads, BLOCK, length), lambda i, s: (0, i + first, 0)),
        ],
        whole((16 * levels, heads * 16)),
        jax.ShapeDtypeStruct((16 * levels, heads * 16), F32),
        [],
        2 * levels * heads * length * length,
        8 * length * length,
        (here, buckets, grads),
        tokens,
        VMEM_MOST,
    )


def table_picked(sums, heads):
    own = jnp.eye(16, dtype=F32)
    by_row = sums.reshape(16, -1, heads, 16) * own[:, None, None, :]
    return jnp.sum(by_row, axis=(0, 3))


def local(
    inputs,
    encoder,
    buckets,
    query_weight,
    key_weight,
    value_weight,
    output_weight,
    crossquery,
    crosskey,
    crossvalue,
    crossoutput,
    gate_weight,
    up_weight,
    down_weight,
    norm_gains,
    bias_table,
    cotangent,
):
    here_index = lax.axis_index("tensor")
    here = here_index.astype(jnp.int32).reshape(1)
    head_local = HEADS // lax.axis_size("tensor")
    head_start = here_index * head_local
    gains = norm_gains[0].astype(F32)
    levels = bias_table.shape[0]
    table_local = lax.dynamic_slice_in_dim(bias_table, head_start, head_local, 1)
    table_rows = jnp.zeros((8, 128), F32).at[:head_local, :levels].set(table_local.T.astype(F32))

    residual = inputs.astype(F32)
    packed = pack(here, "pack_self", (query_weight, key_weight, value_weight, output_weight))
    normed = normalize(residual, gains[0]).astype(BF)
    bias = make_bias(here, buckets, table_rows, head_local)
    packed_cross = pack(here, "pack_cross", (crossquery, crosskey, crossvalue, crossoutput))
    packed_ff = pack(here, "pack_ff", (gate_weight, up_weight, down_weight))
    rows_self = gather_rows(normed)
    memory = gather_rows(encoder)
    grad_out = gather_rows(cotangent)
    gathering = Gathering(packed)
    gathering.step(normed, packed_cross)
    gathering.step(bias, rows_self[3], memory[1])
    sent_self = gathering.held[0]
    gathering.step(grad_out[1], packed_ff)
    (weights_self,) = gathering.finish()
    gathering_cross = Gathering(after(packed_cross, sent_self))
    gathering_cross.step(weights_self)
    gathering_ff = Gathering(packed_ff)

    queries, keys, values, shares, mixture, send, keep = self_forward(
        here, rows_self, weights_self, bias, (gathering_cross.held[0],)
    )
    gathering_cross.step(send)
    first, outgoing = start_sums(after(send, gathering_cross.held[0]), keep)
    gathering_ff.held = [after(packed_ff, gathering_cross.held[0])]
    gathering_ff.step(outgoing)
    gathering_cross.step(outgoing)
    (weights_cross,) = gathering_cross.finish()
    middle = residual + finish_sums(first, outgoing)

    projected = []

    def project_memory(token):
        projected.extend(cross_projections(here, memory, weights_cross, (token,)))
        return (projected[0], gathering_ff.held[0])

    rows_cross = gather_rows(normalize(middle, gains[1]).astype(BF), project_memory)
    cross_keys, cross_values = projected
    cross_queries, cross_shares, cross_mixture, send, keep = cross_forward(
        here, rows_cross, weights_cross, cross_keys, cross_values, ()
    )
    gathering_ff.step(send, split=True)
    first, outgoing = start_sums(after(send, *gathering_ff.held), keep)
    gathering_ff.step(outgoing, part=0)
    gathering_ff.step(outgoing, part=1)
    late = middle + finish_sums(first, outgoing, *gathering_ff.held[:2])

    gathering_ff.step(part=2)
    rows_ff = gather_rows(
        normalize(late, gains[2]).astype(BF), lambda token: (gathering_ff.held[2],)
    )
    weights_ff = gathering_ff.finish()
    hidden, grad_gate, grad_up, send, keep = feed_forward(here, rows_ff, grad_out, weights_ff)
    first, outgoing = start_sums(send, keep)
    send_ff, keep_ff = weight_grads(
        "grads_ff", ((rows_ff, (grad_gate, grad_up)), (grad_out, (hidden,))), (outgoing,)
    )
    reduce_ff = [Reduction(send_ff[n : n + 1], keep_ff[n : n + 1]) for n in range(3)]
    dn = finish_sums(first, outgoing, send_ff)
    back, gain_ff = normalize_back(late, gains[2], dn)
    grad_flow = cotangent.astype(F32) + back

    down = []

    def project_down(token):
        down.extend(down_projection(here, hidden, weights_ff[2], (token,)))
        reduce_ff[0].step(token)
        return (down[0], reduce_ff[0].send)

    grad_late = gather_rows(grad_flow.astype(BF), project_down)
    cross_dq, cross_dk, cross_dv, send, keep = cross_backward(
        here, grad_late, weights_cross, cross_shares, cross_queries, cross_keys, cross_values
    )
    reduce_ff[1].step(send)
    first, outgoing = start_sums(after(send, reduce_ff[1].send), keep)
    reduce_ff[2].step(outgoing)
    reduce_cross = Reduction(
        *weight_grads(
            "grads_cross",
            (
                (rows_cross, (cross_dq,)),
                (memory, (cross_dk, cross_dv)),
                (grad_late, (cross_mixture,)),
            ),
            (outgoing,),
        )
    )
    dn = finish_sums(first, outgoing, reduce_cross.send, reduce_ff[2].send)
    back, gain_cross = normalize_back(middle, gains[1], dn)
    grad_flow = grad_flow + back

    memory_sums = []

    def project_sources(token):
        memory_sums.extend(memory_grads(here, cross_dk, cross_dv, weights_cross, (token,)))
        return memory_sums[:1]

    grad_middle = gather_rows(grad_flow.astype(BF), project_sources)
    reduce_ff = Reduction.joined(reduce_ff)
    first_out, outgoing_out = start_sums(*down)
    first_memory, outgoing_memory = start_sums(*memory_sums)
    dq, dk, dv, ds, send, keep = self_backward(
        here,
        grad_middle,
        weights_self,
        shares,
        queries,
        keys,
        values,
        (outgoing_out, outgoing_memory, reduce_ff.send),
    )
    outputs = (late + finish_sums(first_out, outgoing_out)).astype(BF)
    reduce_ff.step(send)
    reduce_cross.step(send)
    first, outgoing = start_sums(after(send, reduce_ff.send, reduce_cross.send), keep)
    reduce_self = Reduction(
        *weight_grads(
            "grads_self", ((rows_self, (dq, dk, dv)), (grad_middle, (mixture,))), (outgoing,)
        )
    )
    dn = finish_sums(first, outgoing, reduce_self.send)
    back, gain_self = normalize_back(residual, gains[0], dn)
    grad_flow = grad_flow + back
    blocks = buckets.shape[0] // BLOCK
    early = blocks - 1
    raw = table_sums(here, buckets, ds, levels, 0, early, (gain_self,))
    reduce_self.step(raw)
    reduce_cross.step(raw)
    grad_encoder = finish_sums(first_memory, after(outgoing_memory, dn), raw)
    raw_late = table_sums(
        here, buckets, ds, levels, early, blocks - early, (reduce_self.send, reduce_cross.send)
    )
    reduce_self.step(raw_late)
    grads_cross = reduce_cross.finish(raw_late)
    grads_ff = reduce_ff.finish(raw_late)
    raw = raw + after(raw_late, *([reduce_self.send] if reduce_self.send is not None else []))
    table_part = table_picked(raw, head_local)
    grads_self = reduce_self.finish(raw_late)
    table_full = lax.dynamic_update_slice_in_dim(
        jnp.zeros(bias_table.shape, F32), table_part, head_start, 1
    )
    small = jnp.concatenate(
        [jnp.stack([gain_self, gain_cross, gain_ff]).reshape(-1), table_full.reshape(-1)]
    ).reshape(-1, 128)
    small = sum_everywhere(small, grads_self).reshape(-1)
    gain_size = norm_gains.size
    gain_sums = small[:gain_size].reshape(norm_gains.shape)
    table_full = small[gain_size:].reshape(bias_table.shape)

    return (
        outputs,
        grad_flow,
        grad_encoder,
        grads_self[0:1],
        grads_self[1:2],
        grads_self[2:3],
        grads_self[3].T[None],
        grads_cross[0:1],
        grads_cross[1:2],
        grads_cross[2:3],
        grads_cross[3].T[None],
        grads_ff[0:1],
        grads_ff[1:2],
        grads_ff[2].T[None],
        gain_sums,
        table_full,
    )


def solution(mesh):
    rows = P(("dp", "tensor"), None)
    column = P(None, "dp", "tensor")
    row = P(None, "tensor", "dp")
    weights = (column, column, column, row, column, column, column, row, column, column, row)
    in_specs = (rows, rows, P()) + weights + (P(), P(), rows)
    out_specs = (rows, rows, rows) + weights + (P(), P())
    return jax.shard_map(local, mesh=mesh, in_specs=in_specs, out_specs=out_specs, check_vma=False)
```

```python
import jax
import jax.numpy as jnp
from jax import lax
from jax.experimental import pallas as pl
from jax.experimental.pallas import tpu as pltpu
from jax.sharding import PartitionSpec as P

HEADS = 12
HEAD_DIM = 64
EPS = 1e-06
BF = jnp.bfloat16
F32 = jnp.float32
BLOCK = 256
VMEM_LIMIT = 40 * 1024 * 1024
VMEM_MOST = 60 * 1024 * 1024
FLOP_PER_US = 1.15e9
EXPECTED_US = {
    "pack_self": 1.6,
    "pack_cross": 1.6,
    "pack_ff": 1.8,
    "position_bias": 8,
    "self_forward": 10,
    "cross_projections": 1.6,
    "cross_forward": 7,
    "feed_forward": 7,
    "down_projection": 2,
    "cross_backward": 10,
    "grads_ff": 4,
    "grads_cross": 4,
    "memory_grads": 1,
    "self_backward": 14,
    "grads_self": 3.5,
    "table_sums": 14,
}

CORE = [(0, 1), (1, 0), (2, 3), (3, 2)]
CHIP = [(0, 2), (2, 0), (1, 3), (3, 1)]
SEND_FIRST = (2, 3, 0, 1)


def after(value, *others):
    return lax.optimization_barrier((value,) + others)[0]


def gather_rows(piece, meanwhile=None):
    far = lax.ppermute(piece, "tensor", CHIP)
    near = lax.ppermute(piece, "tensor", CORE)
    if meanwhile is not None:
        far = after(far, *meanwhile(piece))
    last = lax.ppermute(far, "tensor", CORE)
    return (piece, far, near, last)


def start_sums(send, keep):
    rows = keep.shape[0] // 2
    near = lax.ppermute(send, "tensor", CORE)
    outgoing = (keep[rows:].astype(F32) + near[rows:].astype(F32)).astype(BF)
    return (keep, near), outgoing


def finish_sums(first, outgoing, *meanwhile):
    keep, near = first
    rows = outgoing.shape[0]
    far = lax.ppermute(outgoing, "tensor", CHIP)
    if meanwhile:
        far = after(far, *meanwhile)
    return keep[:rows].astype(F32) + near[:rows].astype(F32) + far.astype(F32)


def swap_pairs(size, bit):
    return [(i, i ^ bit) for i in range(size)]


class Gathering:

    def __init__(self, shard):
        self.held = [shard]
        self.axis = 1
        self.bit = lax.axis_size("dp") // 2

    def step(self, *waits, part=None, split=0):
        size = lax.axis_size("dp")
        second = (lax.axis_index("dp") & self.bit) != 0
        parts = []
        for number, held in enumerate(self.held):
            if part is not None and number != part:
                parts.append(held)
                continue
            other = lax.ppermute(held, "dp", swap_pairs(size, self.bit))
            if waits:
                other = after(other, *waits)
            for low in range(0, held.shape[0], split or held.shape[0]):
                pick = slice(low, low + (split or held.shape[0]))
                mine, theirs = held[pick], other[pick]
                parts.append(
                    jnp.stack(
                        [jnp.where(second, theirs, mine), jnp.where(second, mine, theirs)],
                        axis=self.axis,
                    )
                )
        self.held = parts
        if part is None or part == len(parts) - 1:
            self.axis += 1
            self.bit //= 2

    def finish(self):
        while self.bit >= 1:
            self.step()
        return [held.reshape(held.shape[0], -1, held.shape[-1]) for held in self.held]


class Reduction:

    def __init__(self, send, keep):
        self.send, self.keep, self.total = send, keep, None
        self.bit = 1
        self.shape = keep.shape

    def step(self, *waits):
        size = lax.axis_size("dp")
        me = lax.axis_index("dp")
        received = lax.ppermute(self.send, "dp", swap_pairs(size, self.bit))
        if waits:
            received = after(received, *waits)
        current = self.keep.astype(F32) + received.astype(F32)
        self.bit *= 2
        count, _, rows, columns = self.shape
        self.send = self.keep = None
        if self.bit >= size:
            self.total = current.reshape(count, rows, columns)
            return
        current = current.reshape(count, size // (2 * self.bit), 2, rows, columns)
        mine = jnp.where((me & self.bit) != 0, 1, 0)
        self.send = lax.dynamic_index_in_dim(current, 1 - mine, 2, keepdims=False).astype(BF)
        self.keep = lax.dynamic_index_in_dim(current, mine, 2, keepdims=False)

    @staticmethod
    def joined(parts):
        whole_sum = Reduction(
            jnp.concatenate([part.send for part in parts]),
            jnp.concatenate([part.keep for part in parts]),
        )
        whole_sum.bit = parts[0].bit
        whole_sum.shape = (sum(part.shape[0] for part in parts),) + parts[0].shape[1:]
        return whole_sum

    def finish(self, *waits):
        while self.send is not None:
            self.step(*waits)
        return self.total


def sum_everywhere(values):
    for pairs in (CORE, CHIP):
        values = values + lax.ppermute(values, "tensor", pairs)
    size = lax.axis_size("dp")
    bit = 1
    while bit < size:
        values = values + lax.ppermute(values, "dp", swap_pairs(size, bit))
        bit *= 2
    return values


def dot_nn(left, right):
    return jnp.dot(left, right, preferred_element_type=F32)


def dot_nt(left, right):
    return lax.dot_general(left, right, (((1,), (1,)), ((), ())), preferred_element_type=F32)


def dot_tn(left, right):
    return lax.dot_general(left, right, (((0,), (0,)), ((), ())), preferred_element_type=F32)


def normalize(values, gain_row):
    inverse_root = lax.rsqrt(jnp.mean(values * values, axis=-1, keepdims=True) + EPS)
    return values * inverse_root * gain_row


def normalize_back(values, gain_row, grad):
    inverse_root = lax.rsqrt(jnp.mean(values * values, axis=-1, keepdims=True) + EPS)
    scaled = values * inverse_root
    gain_grad = jnp.sum(grad * scaled, axis=0)
    inner = grad * gain_row
    back = inverse_root * (inner - scaled * jnp.mean(inner * scaled, axis=-1, keepdims=True))
    return back, gain_grad


def row_place(block, here):
    turned = lax.bitwise_xor(block, here)
    return lax.bitwise_or(
        lax.shift_left(lax.bitwise_and(turned, 1), 1), lax.shift_right_logical(turned, 1)
    )


def head_masks(rows, columns):
    lane_head = lax.broadcasted_iota(jnp.int32, (rows, columns), 1) // HEAD_DIM
    return [lane_head == head for head in range(columns // HEAD_DIM)]


def only(mask, values):
    return jnp.where(mask, values, jnp.zeros_like(values))


def call(kernel, name, grid, in_specs, out_specs, out_shape, scratch, flops, moved, args, tokens=(), limit=VMEM_LIMIT):
    inputs = 1 + len(in_specs)

    def run(*refs):
        kernel(*refs[:inputs], *refs[inputs + len(tokens) :])

    return pl.pallas_call(
        run,
        grid_spec=pltpu.PrefetchScalarGridSpec(
            num_scalar_prefetch=1,
            grid=grid,
            in_specs=list(in_specs) + [pl.BlockSpec(memory_space=pl.ANY)] * len(tokens),
            out_specs=out_specs,
            scratch_shapes=scratch,
        ),
        out_shape=out_shape,
        compiler_params=pltpu.CompilerParams(
            dimension_semantics=("arbitrary",) * len(grid), vmem_limit_bytes=limit
        ),
        cost_estimate=pl.CostEstimate(
            flops=int(EXPECTED_US[name] * FLOP_PER_US), bytes_accessed=1, transcendentals=0
        ),
        name=name,
    )(*args, *tokens)


def whole(shape):
    return pl.BlockSpec(shape, lambda i, s: (0,) * len(shape))


def member(index, shape):
    return pl.BlockSpec((None,) + shape, lambda i, s: (index,) + (0,) * len(shape))


def turn(step):
    return lax.rem(step + 2, 4)


def quarter_spec(columns):
    return pl.BlockSpec((BLOCK, columns), lambda i, s: (turn(i), 0))


def piece_specs(pieces):
    return [whole(piece.shape) for piece in pieces]


def half_specs(width):
    return [
        pl.BlockSpec((BLOCK, width), lambda i, s: (jnp.minimum(i, 1), 0)),
        pl.BlockSpec((BLOCK, width), lambda i, s: (jnp.maximum(i - 2, 0), 0)),
    ]


def half_shapes(width):
    return [jax.ShapeDtypeStruct((2 * BLOCK, width), BF)] * 2


def store_half(step, send_ref, keep_ref, values):
    @pl.when(step < 2)
    def _():
        send_ref[...] = values

    @pl.when(step >= 2)
    def _():
        keep_ref[...] = values


def take_quarter(step, refs, target):
    for number, quarter in enumerate(SEND_FIRST):

        @pl.when(step == number)
        def _(quarter=quarter):
            target[...] = refs[quarter][...]


def pack_kernel(here_ref, *refs):
    packed_ref = refs[-1]
    columns = refs[0].shape[2]
    for number, ref in enumerate(refs[:-1]):
        values = ref[0] if number < len(refs) - 2 else ref[0].T
        if len(packed_ref.shape) == 3:
            packed_ref[number] = values
        else:
            packed_ref[:, number * columns : (number + 1) * columns] = values


def pack(here, name, matrices, flat=False):
    rows, columns = matrices[0].shape[1:]
    shape = (rows, len(matrices) * columns) if flat else (len(matrices), rows, columns)
    if rows % 16:
        turned = list(matrices[:-1]) + [matrices[-1].transpose(0, 2, 1)]
        return jnp.concatenate(turned, axis=2)[0] if flat else jnp.concatenate(turned)
    return call(
        pack_kernel,
        name,
        (1,),
        [whole(matrix.shape) for matrix in matrices],
        whole(shape),
        jax.ShapeDtypeStruct(shape, BF),
        [],
        0,
        0,
        (here, *matrices),
        limit=VMEM_MOST,
    )


def bias_kernel(here_ref, buckets_ref, table_ref, bias_ref):
    block = pl.program_id(0)
    heads = bias_ref.shape[0]
    length = buckets_ref.shape[1]
    for column in range(length // 128):

        @pl.when(column * 128 < (block + 1) * BLOCK)
        def _():
            lanes = slice(column * 128, (column + 1) * 128)
            ids = buckets_ref[:, lanes]
            for head in range(heads):
                row = jnp.broadcast_to(table_ref[head : head + 1, :], ids.shape)
                picked = jnp.take_along_axis(row, ids, axis=1, mode="promise_in_bounds")
                bias_ref[head, :, lanes] = picked.astype(BF)


def make_bias(here, buckets, table_rows, heads, tokens):
    length = buckets.shape[0]
    blocks = length // BLOCK
    return call(
        bias_kernel,
        "position_bias",
        (blocks,),
        [pl.BlockSpec((BLOCK, length), lambda i, s: (i, 0)), whole(table_rows.shape)],
        pl.BlockSpec((heads, BLOCK, length), lambda i, s: (0, i, 0)),
        jax.ShapeDtypeStruct((heads, length, length), BF),
        [],
        0,
        12 * length * length,
        (here, buckets, table_rows),
        tokens,
        VMEM_MOST,
    )


def self_kernel(
    here_ref, *refs
):
    pieces = refs[:4]
    w_ref, bias_ref, q_ref, k_ref, v_ref, share_ref, mix_ref, send_ref, keep_ref = refs[4:]
    block = pl.program_id(0)
    here = here_ref[0]
    length, width = q_ref.shape
    masks = head_masks(BLOCK, width)

    @pl.when(block == 0)
    def _():
        for quarter, piece in enumerate(pieces):
            rows = piece[...]
            place = slice(quarter * BLOCK, (quarter + 1) * BLOCK)
            for number, target in enumerate((q_ref, k_ref, v_ref)):
                target[place, :] = dot_nn(rows, w_ref[number]).astype(BF)

    def one(index):
        def at(quarter):
            return pl.ds(pl.multiple_of(row_place(quarter, here) * BLOCK, BLOCK), BLOCK)

        queries = q_ref[at(index), :]
        keys = [k_ref[at(other), :] for other in range(index + 1)]
        values = [v_ref[at(other), :] for other in range(index + 1)]
        visible = lax.broadcasted_iota(jnp.int32, (BLOCK, BLOCK), 1) <= lax.broadcasted_iota(
            jnp.int32, (BLOCK, BLOCK), 0
        )
        mixture = jnp.zeros((BLOCK, width), F32)
        for head, mask in enumerate(masks):
            own = only(mask, queries)
            scores = []
            for other in range(index + 1):
                lanes = slice(other * BLOCK, (other + 1) * BLOCK)
                score = dot_nt(own, keys[other]) + bias_ref[head, :, lanes].astype(F32)
                if other == index:
                    score = jnp.where(visible, score, -1000000000.0)
                scores.append(score)
            highest = scores[0]
            for score in scores[1:]:
                highest = jnp.maximum(highest, score)
            highest = jnp.max(highest, axis=-1, keepdims=True)
            raised = [jnp.exp(score - highest) for score in scores]
            total = raised[0]
            for part in raised[1:]:
                total = total + part
            inverse = 1.0 / jnp.sum(total, axis=-1, keepdims=True)
            mixed = None
            for other in range(index + 1):
                lanes = slice(other * BLOCK, (other + 1) * BLOCK)
                share = (raised[other] * inverse).astype(BF)
                share_ref[head, :, lanes] = share
                part = dot_nn(share, values[other])
                mixed = part if mixed is None else mixed + part
            mixture = mixture + only(mask, mixed)
        mix_ref[at(index), :] = mixture.astype(BF)

    for index in range(length // BLOCK):
        pl.when(block == index)(lambda index=index: one(index))

    @pl.when(block == length // BLOCK - 1)
    def _():
        half = length // 2
        for quarter in range(2):
            place = slice(quarter * BLOCK, (quarter + 1) * BLOCK)
            away = slice(half + quarter * BLOCK, half + (quarter + 1) * BLOCK)
            send_ref[place, :] = dot_nt(mix_ref[away, :], w_ref[3]).astype(BF)
            keep_ref[place, :] = dot_nt(mix_ref[place, :], w_ref[3]).astype(BF)


def self_forward(here, pieces, weights, bias, tokens):
    heads, length, _ = bias.shape
    width, columns = weights.shape[1:]
    blocks = length // BLOCK
    whole_rows = jax.ShapeDtypeStruct((length, columns), BF)
    square_spec = pl.BlockSpec((heads, BLOCK, length), lambda i, s: (0, i, 0))
    return call(
        self_kernel,
        "self_forward",
        (blocks,),
        piece_specs(pieces) + [whole(weights.shape), square_spec],
        [whole((length, columns))] * 3
        + [square_spec, whole((length, columns))]
        + [whole((length // 2, width))] * 2,
        [whole_rows] * 3
        + [jax.ShapeDtypeStruct((heads, length, length), BF), whole_rows]
        + half_shapes(width),
        [],
        2 * length * width * columns * 4 + 16 * heads * length * length * HEAD_DIM,
        16 * length * length,
        (here, *pieces, weights, bias),
        tokens,
    )


def cross_keys_kernel(here_ref, *refs):
    pieces = refs[:4]
    wk_ref, wv_ref, k_ref, v_ref = refs[4:]
    rows = pieces[0].shape[0]
    for quarter, piece in enumerate(pieces):
        place = slice(quarter * rows, (quarter + 1) * rows)
        values = piece[...]
        k_ref[place, :] = dot_nn(values, wk_ref[...]).astype(BF)
        v_ref[place, :] = dot_nn(values, wv_ref[...]).astype(BF)


def cross_projections(here, pieces, weights, tokens):
    rows, width = pieces[0].shape
    columns = weights.shape[2]
    shape = (4 * rows, columns)
    return call(
        cross_keys_kernel,
        "cross_projections",
        (1,),
        piece_specs(pieces) + [member(1, (width, columns)), member(2, (width, columns))],
        [whole(shape)] * 2,
        [jax.ShapeDtypeStruct(shape, BF)] * 2,
        [],
        16 * rows * width * columns,
        16 * rows * width,
        (here, *pieces, weights, weights),
        tokens,
    )


def cross_kernel(here_ref, *refs):
    pieces = refs[:4]
    w_ref, wo_ref, k_ref, v_ref, q_ref, share_ref, mix_ref, send_ref, keep_ref, rows_ref = refs[4:]
    step = pl.program_id(0)
    width = q_ref.shape[1]
    masks = head_masks(BLOCK, width)
    take_quarter(step, pieces, rows_ref)
    queries = dot_nn(rows_ref[...], w_ref[...]).astype(BF)
    q_ref[...] = queries
    keys = k_ref[...]
    values = v_ref[...]
    mixture = jnp.zeros((BLOCK, width), F32)
    for head, mask in enumerate(masks):
        scores = dot_nt(only(mask, queries), keys)
        raised = jnp.exp(scores - jnp.max(scores, axis=-1, keepdims=True))
        share = (raised * (1.0 / jnp.sum(raised, axis=-1, keepdims=True))).astype(BF)
        share_ref[head] = share
        mixture = mixture + only(mask, dot_nn(share, values))
    mixture = mixture.astype(BF)
    mix_ref[...] = mixture
    store_half(step, send_ref, keep_ref, dot_nt(mixture, wo_ref[...]).astype(BF))


def cross_forward(here, pieces, weights, keys, values, tokens):
    width, columns = weights.shape[1:]
    length = 4 * BLOCK
    heads = columns // HEAD_DIM
    sources = keys.shape[0]
    whole_rows = jax.ShapeDtypeStruct((length, columns), BF)
    row_spec = quarter_spec(columns)
    return call(
        cross_kernel,
        "cross_forward",
        (4,),
        piece_specs(pieces)
        + [
            member(0, (width, columns)),
            member(3, (width, columns)),
            whole((sources, columns)),
            whole((sources, columns)),
        ],
        [row_spec, pl.BlockSpec((heads, BLOCK, sources), lambda i, s: (0, turn(i), 0)), row_spec]
        + half_specs(width),
        [whole_rows, jax.ShapeDtypeStruct((heads, length, sources), BF), whole_rows]
        + half_shapes(width),
        [pltpu.VMEM((BLOCK, width), BF)],
        4 * length * width * columns + 16 * heads * length * sources * HEAD_DIM,
        8 * length * length,
        (here, *pieces, weights, weights, keys, values),
        tokens,
    )


def ff_kernel(here_ref, *refs):
    pieces = refs[:4]
    grads = refs[4:8]
    w_gate_ref, w_up_ref, w_down_ref = refs[8:11]
    hidden_ref, grad_gate_ref, grad_up_ref, send_ref, keep_ref, rows_ref, back_ref = refs[11:]
    step = pl.program_id(0)
    take_quarter(step, pieces, rows_ref)
    take_quarter(step, grads, back_ref)
    rows = rows_ref[...]
    gate = dot_nn(rows, w_gate_ref[0])
    up = dot_nn(rows, w_up_ref[0])
    grad = dot_nn(back_ref[...], w_down_ref[0])
    slope = 0.7978845608028654
    square = gate * gate
    bent = jnp.tanh(slope * (gate + 0.044715 * (square * gate)))
    half = 0.5 * (1.0 + bent)
    active = gate * half
    change = half + 0.5 * gate * (1.0 - bent * bent) * slope * (1.0 + 3.0 * 0.044715 * square)
    hidden_ref[...] = (active * up).astype(BF)
    grad_gate = (grad * up * change).astype(BF)
    grad_up = (grad * active).astype(BF)
    grad_gate_ref[...] = grad_gate
    grad_up_ref[...] = grad_up
    dn = dot_nt(grad_gate, w_gate_ref[0]) + dot_nt(grad_up, w_up_ref[0])
    store_half(step, send_ref, keep_ref, dn.astype(BF))


def feed_forward(here, pieces, grads, weights):
    width, columns = weights[0].shape[1:]
    length = 4 * BLOCK
    row_spec = quarter_spec(columns)
    whole_rows = jax.ShapeDtypeStruct((length, columns), BF)
    return call(
        ff_kernel,
        "feed_forward",
        (4,),
        piece_specs(pieces) + piece_specs(grads) + piece_specs(weights),
        [row_spec] * 3 + half_specs(width),
        [whole_rows] * 3 + half_shapes(width),
        [pltpu.VMEM((BLOCK, width), BF), pltpu.VMEM((BLOCK, width), BF)],
        10 * length * width * columns,
        12 * length * width,
        (here, *pieces, *grads, *weights),
    )


def down_kernel(here_ref, hidden_ref, w_ref, send_ref, keep_ref):
    step = pl.program_id(0)
    store_half(step, send_ref, keep_ref, dot_nt(hidden_ref[...], w_ref[...]).astype(BF))


def down_projection(here, hidden, weights, tokens):
    width, columns = weights.shape[1:]
    length = 4 * BLOCK
    return call(
        down_kernel,
        "down_projection",
        (4,),
        [quarter_spec(columns), member(0, (width, columns))],
        half_specs(width),
        half_shapes(width),
        [],
        2 * length * width * columns,
        6 * length * width,
        (here, hidden, weights),
        tokens,
    )


def weight_grads_kernel(plan, split, apart, bit_ref, *refs):
    pieces = max(first for first, _ in plan) + 4
    grads = max(number for _, number in plan) + 1
    piece_refs, refs = refs[:pieces], refs[pieces:]
    grad_refs, refs = refs[:grads], refs[grads:]
    bit = bit_ref[0]
    turned = {}
    for slot, (first, number) in enumerate(plan):
        if first not in turned:
            turned = {first: [piece_refs[first + part][...].T for part in range(4)]}
        grad_ref = grad_refs[number]
        rows = turned[first][0].shape[1]
        summed = None
        for part in range(4):
            place = slice(part * rows, (part + 1) * rows)
            addend = dot_nn(turned[first][part], grad_ref[place, :])
            summed = addend if summed is None else summed + addend
        if not split:
            start = sum(grad_refs[earlier].shape[1] for _, earlier in plan[:slot])
            refs[0][:, start : start + grad_ref.shape[1]] = summed.astype(BF)
            continue
        if apart:
            send_ref, keep_ref, sum_ref = refs[2 * slot], refs[2 * slot + 1], refs[-1]
            slot = 0
        else:
            send_ref, keep_ref, sum_ref = refs
        sum_ref[...] = summed
        half, block = send_ref.shape[1:3]
        for number_here in range(half):
            for target, side in ((send_ref, 1 - bit), (keep_ref, bit)):
                start = pl.multiple_of((2 * number_here + side) * block, block)
                target[slot, number_here] = sum_ref[pl.ds(start, block), :].astype(BF)


def weight_grads(name, groups, tokens=(), apart=False):
    size = lax.axis_size("dp")
    bit = lax.bitwise_and(lax.axis_index("dp").astype(jnp.int32), 1)
    plan = []
    pieces = []
    grads = []
    for group, arrays in groups:
        for array in arrays:
            plan.append((len(pieces), len(grads)))
            grads.append(array)
        pieces.extend(group)
    width = pieces[0].shape[1]
    columns = grads[0].shape[1]
    block = width // size
    split = block % 16 == 0
    if split:
        shapes = [(len(plan), size // 2, block, columns)] * 2
        if apart:
            shapes = [(1, size // 2, block, columns)] * (2 * len(plan))
    else:
        shapes = [(width, sum(grad.shape[1] for grad in grads))]
    out = call(
        lambda *refs: weight_grads_kernel(tuple(plan), split, apart, *refs),
        name,
        (1,),
        [whole(piece.shape) for piece in pieces] + [whole(grad.shape) for grad in grads],
        [whole(shape) for shape in shapes],
        [jax.ShapeDtypeStruct(shape, BF) for shape in shapes],
        [pltpu.VMEM((width, columns), F32)] if split else [],
        sum(2 * grad.shape[0] * width * columns for grad in grads),
        4 * len(plan) * width * columns,
        (bit.reshape(1), *pieces, *grads),
        tokens,
        VMEM_LIMIT if name == "grads_self" else VMEM_MOST,
    )
    if split:
        return list(zip(out[0::2], out[1::2])) if apart else out
    halves = out[0].reshape(size // 2, 2, block, len(plan), columns).transpose(3, 0, 1, 2, 4)
    send, keep = [
        lax.dynamic_index_in_dim(halves, side, 2, keepdims=False) for side in (1 - bit, bit)
    ]
    if apart:
        return [(send[n : n + 1], keep[n : n + 1]) for n in range(len(plan))]
    return send, keep


def cross_back_kernel(here_ref, *refs):
    pieces = refs[:4]
    w_out_ref, w_q_ref, share_ref, q_ref, k_ref, v_ref = refs[4:10]
    dq_ref, dk_ref, dv_ref, send_ref, keep_ref, dk_sum, dv_sum, rows_ref = refs[10:]
    step = pl.program_id(0)
    width = q_ref.shape[1]
    masks = head_masks(BLOCK, width)
    take_quarter(step, pieces, rows_ref)
    grad = dot_nn(rows_ref[...], w_out_ref[...]).astype(BF)
    queries = q_ref[...]
    keys = k_ref[...]
    values = v_ref[...]

    @pl.when(step == 0)
    def _():
        dk_sum[...] = jnp.zeros_like(dk_sum)
        dv_sum[...] = jnp.zeros_like(dv_sum)

    dq = jnp.zeros((BLOCK, width), F32)
    dk = dk_sum[...]
    dv = dv_sum[...]
    for head, mask in enumerate(masks):
        own_grad = only(mask, grad)
        low = share_ref[head]
        share = low.astype(F32)
        weighted = dot_nt(own_grad, values) * share
        inner = jnp.sum(weighted, axis=-1, keepdims=True)
        grad_low = (weighted - share * inner).astype(BF)
        dq = dq + only(mask, dot_nn(grad_low, keys))
        dk = dk + dot_tn(grad_low, only(mask, queries))
        dv = dv + dot_tn(low, own_grad)
    dk_sum[...] = dk
    dv_sum[...] = dv
    dq = dq.astype(BF)
    dq_ref[...] = dq
    store_half(step, send_ref, keep_ref, dot_nt(dq, w_q_ref[...]).astype(BF))

    @pl.when(step == pl.num_programs(0) - 1)
    def _():
        dk_ref[...] = dk.astype(BF)
        dv_ref[...] = dv.astype(BF)


def cross_backward(here, pieces, weights, shares, queries, keys, values):
    width, columns = weights.shape[1:]
    length = 4 * BLOCK
    heads = columns // HEAD_DIM
    sources = keys.shape[0]
    row_spec = quarter_spec(columns)
    source_spec = whole((sources, columns))
    source_shape = jax.ShapeDtypeStruct((sources, columns), BF)
    return call(
        cross_back_kernel,
        "cross_backward",
        (4,),
        piece_specs(pieces)
        + [
            member(3, (width, columns)),
            member(0, (width, columns)),
            pl.BlockSpec((heads, BLOCK, sources), lambda i, s: (0, turn(i), 0)),
            row_spec,
            source_spec,
            source_spec,
        ],
        [row_spec, source_spec, source_spec] + half_specs(width),
        [jax.ShapeDtypeStruct((length, columns), BF), source_shape, source_shape]
        + half_shapes(width),
        [
            pltpu.VMEM((sources, columns), F32),
            pltpu.VMEM((sources, columns), F32),
            pltpu.VMEM((BLOCK, width), BF),
        ],
        4 * length * width * columns + 32 * heads * length * sources * HEAD_DIM,
        10 * length * length,
        (here, *pieces, weights, weights, shares, queries, keys, values),
    )


def memory_kernel(here_ref, dk_ref, dv_ref, wk_ref, wv_ref, send_ref, keep_ref):
    half = send_ref.shape[0]
    for target, start in ((send_ref, half), (keep_ref, 0)):
        place = slice(start, start + half)
        summed = dot_nt(dk_ref[place, :], wk_ref[...]) + dot_nt(dv_ref[place, :], wv_ref[...])
        target[...] = summed.astype(BF)


def memory_grads(here, dk, dv, weights, tokens):
    width, columns = weights.shape[1:]
    sources = dk.shape[0]
    half = (sources // 2, width)
    return call(
        memory_kernel,
        "memory_grads",
        (1,),
        [whole(dk.shape)] * 2 + [member(1, (width, columns)), member(2, (width, columns))],
        [whole(half)] * 2,
        [jax.ShapeDtypeStruct(half, BF)] * 2,
        [],
        4 * sources * width * columns,
        4 * sources * width,
        (here, dk, dv, weights, weights),
        tokens,
    )


def self_back_kernel(here_ref, *refs):
    pieces = refs[:4]
    w_ref, share_ref, q_ref, k_ref, v_ref = refs[4:9]
    dq_ref, dk_ref, dv_ref, ds_ref, send_ref, keep_ref, dk_sum, dv_sum, grad_all = refs[9:]
    block = pl.program_id(0)
    here = here_ref[0]
    length, width = q_ref.shape
    count = length // BLOCK
    masks = head_masks(BLOCK, width)

    @pl.when(block == 0)
    def _():
        dk_sum[...] = jnp.zeros_like(dk_sum)
        dv_sum[...] = jnp.zeros_like(dv_sum)
        for quarter, piece in enumerate(pieces):
            place = slice(quarter * BLOCK, (quarter + 1) * BLOCK)
            grad_all[place, :] = dot_nn(piece[...], w_ref[3]).astype(BF)

    def one(index):
        def at(quarter):
            return pl.ds(pl.multiple_of(row_place(quarter, here) * BLOCK, BLOCK), BLOCK)

        grad = grad_all[at(index), :]
        queries = q_ref[at(index), :]
        dq = jnp.zeros((BLOCK, width), F32)
        for head, mask in enumerate(masks):
            own_grad = only(mask, grad)
            own_query = only(mask, queries)
            shares = []
            weighted = []
            for other in range(index + 1):
                lanes = slice(other * BLOCK, (other + 1) * BLOCK)
                low = share_ref[head, :, lanes]
                shares.append(low)
                weighted.append(dot_nt(own_grad, v_ref[at(other), :]) * low.astype(F32))
            inner = weighted[0]
            for part in weighted[1:]:
                inner = inner + part
            inner = jnp.sum(inner, axis=-1, keepdims=True)
            part_q = None
            for other in range(index + 1):
                lanes = slice(other * BLOCK, (other + 1) * BLOCK)
                low = shares[other]
                grad_low = (weighted[other] - low.astype(F32) * inner).astype(BF)
                ds_ref[head, :, lanes] = grad_low
                part = dot_nn(grad_low, k_ref[at(other), :])
                part_q = part if part_q is None else part_q + part
                dk_sum[at(other), :] += dot_tn(grad_low, own_query)
                dv_sum[at(other), :] += dot_tn(low, own_grad)
            dq = dq + only(mask, part_q)
        dq_ref[at(index), :] = dq.astype(BF)

    for index in range(count):
        pl.when(block == index)(lambda index=index: one(index))

    @pl.when(block == count - 1)
    def _():
        for quarter in range(count):
            place = slice(quarter * BLOCK, (quarter + 1) * BLOCK)
            dk = dk_sum[place, :].astype(BF)
            dv = dv_sum[place, :].astype(BF)
            dk_ref[place, :] = dk
            dv_ref[place, :] = dv
            dn = dot_nt(dq_ref[place, :], w_ref[0]) + dot_nt(dk, w_ref[1]) + dot_nt(dv, w_ref[2])
            target = keep_ref if quarter < 2 else send_ref
            target[slice(quarter % 2 * BLOCK, (quarter % 2 + 1) * BLOCK), :] = dn.astype(BF)


def self_backward(here, pieces, weights, shares, queries, keys, values, tokens):
    heads, length, _ = shares.shape
    width, columns = weights.shape[1:]
    blocks = length // BLOCK
    square_spec = pl.BlockSpec((heads, BLOCK, length), lambda i, s: (0, i, 0))
    rows = whole((length, columns))
    return call(
        self_back_kernel,
        "self_backward",
        (blocks,),
        piece_specs(pieces) + [whole(weights.shape), square_spec, rows, rows, rows],
        [rows, rows, rows, square_spec] + [whole((length // 2, width))] * 2,
        [jax.ShapeDtypeStruct((length, columns), BF)] * 3
        + [jax.ShapeDtypeStruct((heads, length, length), BF)]
        + half_shapes(width),
        [
            pltpu.VMEM((length, columns), F32),
            pltpu.VMEM((length, columns), F32),
            pltpu.VMEM((length, columns), BF),
        ],
        8 * length * width * columns + 20 * heads * length * length * HEAD_DIM,
        16 * length * length,
        (here, *pieces, weights, shares, queries, keys, values),
        tokens,
    )


def table_kernel(first, here_ref, buckets_ref, ds_ref, out_ref):
    step = pl.program_id(0)
    heads = ds_ref.shape[0]
    group = 16
    levels = out_ref.shape[0] // group

    @pl.when(step == 0)
    def _():
        out_ref[...] = jnp.zeros_like(out_ref)

    def one(index):
        keys = (index + 1) * BLOCK
        level_ids = lax.broadcasted_iota(jnp.int32, (group, levels, BLOCK), 1)

        def strip(number, _):
            rows = pl.ds(pl.multiple_of(number * group, group), group)
            total = None
            for start in range(0, keys, BLOCK):
                lanes = slice(start, start + BLOCK)
                ids = buckets_ref[rows, lanes]
                chosen = jnp.where(ids[:, None, :] == level_ids, 1.0, 0.0).astype(BF)
                grads = ds_ref[:, rows, lanes].reshape(heads * group, BLOCK)
                part = dot_nt(chosen.reshape(group * levels, BLOCK), grads)
                total = part if total is None else total + part
            out_ref[...] += total
            return 0

        lax.fori_loop(0, BLOCK // group, strip, 0)

    for index in range(ds_ref.shape[2] // BLOCK):
        pl.when(step + first == index)(lambda index=index: one(index))


def table_sums(here, buckets, grads, levels, first, count, tokens):
    heads, length, _ = grads.shape
    return call(
        lambda *refs: table_kernel(first, *refs),
        "table_sums",
        (count,),
        [
            pl.BlockSpec((BLOCK, length), lambda i, s: (i + first, 0)),
            pl.BlockSpec((heads, BLOCK, length), lambda i, s: (0, i + first, 0)),
        ],
        whole((16 * levels, heads * 16)),
        jax.ShapeDtypeStruct((16 * levels, heads * 16), F32),
        [],
        2 * levels * heads * length * length,
        8 * length * length,
        (here, buckets, grads),
        tokens,
        VMEM_MOST,
    )


def table_picked(sums, heads):
    own = jnp.eye(16, dtype=F32)
    by_row = sums.reshape(16, -1, heads, 16) * own[:, None, None, :]
    return jnp.sum(by_row, axis=(0, 3))


def local(
    inputs,
    encoder,
    buckets,
    query_weight,
    key_weight,
    value_weight,
    output_weight,
    crossquery,
    crosskey,
    crossvalue,
    crossoutput,
    gate_weight,
    up_weight,
    down_weight,
    norm_gains,
    bias_table,
    cotangent,
):
    here_index = lax.axis_index("tensor")
    here = here_index.astype(jnp.int32).reshape(1)
    head_local = HEADS // lax.axis_size("tensor")
    head_start = here_index * head_local
    gains = norm_gains[0].astype(F32)
    levels = bias_table.shape[0]
    table_local = lax.dynamic_slice_in_dim(bias_table, head_start, head_local, 1)
    table_rows = jnp.zeros((8, 128), F32).at[:head_local, :levels].set(table_local.T.astype(F32))

    residual = inputs.astype(F32)
    packed = pack(here, "pack_self", (query_weight, key_weight, value_weight, output_weight))
    normed = normalize(after(inputs, packed).astype(F32), gains[0]).astype(BF)
    packed_cross = pack(here, "pack_cross", (crossquery, crosskey, crossvalue, crossoutput))
    packed_ff = pack(here, "pack_ff", (gate_weight, up_weight, down_weight))
    memory = gather_rows(encoder)
    grad_out = gather_rows(cotangent)
    gathering = Gathering(packed)
    gathering.step(normed, packed_cross)
    bias = make_bias(here, buckets, table_rows, head_local, ())
    rows_self = gather_rows(normed)
    gathering.step(bias, rows_self[3], memory[1], split=2)
    gathering_cross = Gathering(after(packed_cross, *gathering.held))
    gathering.step(part=0)
    gathering_cross.step(gathering.held[0])
    gathering.step(grad_out[1], packed_ff, part=1)
    weights_self = jnp.concatenate(gathering.finish())
    gathering_cross.step()

    queries, keys, values, shares, mixture, send, keep = self_forward(
        here, rows_self, weights_self, bias, (gathering_cross.held[0],)
    )
    gathering_ff = Gathering(after(packed_ff, gathering_cross.held[0]))
    gathering_ff.step(send)
    gathering_cross.step(send)
    (weights_cross,) = gathering_cross.finish()
    first, outgoing = start_sums(after(send, gathering_ff.held[0], weights_cross), keep)
    gathering_ff.step(outgoing, split=1)
    middle = residual + finish_sums(first, outgoing)

    projected = []

    def project_memory(token):
        projected.extend(cross_projections(here, memory, weights_cross, (token,)))
        return projected[:1]

    normed = after(normalize(middle, gains[1]).astype(BF), *gathering_ff.held)
    rows_cross = gather_rows(normed, project_memory)
    gathering_ff.step(normed, part=0)
    cross_keys, cross_values = projected
    cross_queries, cross_shares, cross_mixture, send, keep = cross_forward(
        here, rows_cross, weights_cross, cross_keys, cross_values, (gathering_ff.held[0],)
    )
    first, outgoing = start_sums(send, keep)
    gathering_ff.step(outgoing, part=1)
    late = middle + finish_sums(first, outgoing, gathering_ff.held[1])

    gathering_ff.step(part=2)
    rows_ff = gather_rows(
        normalize(late, gains[2]).astype(BF), lambda token: (gathering_ff.held[2],)
    )
    weights_ff = gathering_ff.finish()
    hidden, grad_gate, grad_up, send, keep = feed_forward(here, rows_ff, grad_out, weights_ff)
    first, outgoing = start_sums(send, keep)
    halves_ff = weight_grads(
        "grads_ff",
        ((rows_ff, (grad_gate, grad_up)), (grad_out, (hidden,))),
        (outgoing,),
        apart=True,
    )
    reduce_ff = [Reduction(*halves) for halves in halves_ff]
    dn = finish_sums(first, outgoing, reduce_ff[0].send)
    back, gain_ff = normalize_back(late, gains[2], dn)
    grad_flow = cotangent.astype(F32) + back

    down = []

    def project_down(token):
        down.extend(down_projection(here, hidden, weights_ff[2], (token,)))
        reduce_ff[0].step(token)
        return (down[0], reduce_ff[0].send)

    grad_late = gather_rows(grad_flow.astype(BF), project_down)
    cross_dq, cross_dk, cross_dv, send, keep = cross_backward(
        here, grad_late, weights_cross, cross_shares, cross_queries, cross_keys, cross_values
    )
    reduce_ff[1].step(send)
    first, outgoing = start_sums(after(send, reduce_ff[1].send), keep)
    reduce_cross = Reduction(
        *weight_grads(
            "grads_cross",
            (
                (rows_cross, (cross_dq,)),
                (memory, (cross_dk, cross_dv)),
                (grad_late, (cross_mixture,)),
            ),
            (outgoing,),
        )
    )
    reduce_ff[2].step(reduce_cross.send)
    dn = finish_sums(first, outgoing, reduce_cross.send)
    back, gain_cross = normalize_back(middle, gains[1], dn)
    grad_flow = grad_flow + back

    memory_sums = []

    def project_sources(token):
        memory_sums.extend(memory_grads(here, cross_dk, cross_dv, weights_cross, (token,)))
        return (memory_sums[0], reduce_ff[2].send)

    grad_middle = gather_rows(grad_flow.astype(BF), project_sources)
    reduce_ff = Reduction.joined(reduce_ff)
    first_out, outgoing_out = start_sums(*down)
    first_memory, outgoing_memory = start_sums(*memory_sums)
    dq, dk, dv, ds, send, keep = self_backward(
        here,
        grad_middle,
        weights_self,
        shares,
        queries,
        keys,
        values,
        (outgoing_out, outgoing_memory, reduce_ff.send),
    )
    reduce_ff.step(send)
    reduce_cross.step(send)
    first, outgoing = start_sums(after(send, reduce_ff.send, reduce_cross.send), keep)
    reduce_self = Reduction(
        *weight_grads(
            "grads_self", ((rows_self, (dq, dk, dv)), (grad_middle, (mixture,))), (outgoing,)
        )
    )
    blocks = buckets.shape[0] // BLOCK
    early = blocks - 1
    raw = table_sums(here, buckets, ds, levels, 0, early, (reduce_self.send,))
    reduce_self.step(raw)
    next_send = raw if reduce_self.send is None else reduce_self.send
    raw_late = table_sums(here, buckets, ds, levels, early, blocks - early, (next_send,))
    if reduce_self.send is not None:
        reduce_self.step(raw_late)
    sent = reduce_self.total if reduce_self.send is None else reduce_self.send
    dn = finish_sums(first, outgoing, sent)
    back, gain_self = normalize_back(residual, gains[0], dn)
    grad_flow = grad_flow + back
    reduce_cross.step(sent)
    outputs = (late + finish_sums(first_out, after(outgoing_out, dn), sent)).astype(BF)
    grad_encoder = finish_sums(first_memory, after(outgoing_memory, dn), sent)
    table_part = table_picked(raw + after(raw_late, sent), head_local)
    grads_cross = reduce_cross.finish(sent)
    grads_ff = reduce_ff.finish(sent)
    grads_self = reduce_self.finish()
    table_full = lax.dynamic_update_slice_in_dim(
        jnp.zeros(bias_table.shape, F32), table_part, head_start, 1
    )
    small = jnp.concatenate(
        [jnp.stack([gain_self, gain_cross, gain_ff]).reshape(-1), table_full.reshape(-1)]
    ).reshape(-1, 128)
    small = sum_everywhere(small).reshape(-1)
    gain_size = norm_gains.size
    gain_sums = small[:gain_size].reshape(norm_gains.shape)
    table_full = small[gain_size:].reshape(bias_table.shape)

    return (
        outputs,
        grad_flow,
        grad_encoder,
        grads_self[0:1],
        grads_self[1:2],
        grads_self[2:3],
        grads_self[3].T[None],
        grads_cross[0:1],
        grads_cross[1:2],
        grads_cross[2:3],
        grads_cross[3].T[None],
        grads_ff[0:1],
        grads_ff[1:2],
        grads_ff[2].T[None],
        gain_sums,
        table_full,
    )


def solution(mesh):
    rows = P(("dp", "tensor"), None)
    column = P(None, "dp", "tensor")
    row = P(None, "tensor", "dp")
    weights = (column, column, column, row, column, column, column, row, column, column, row)
    in_specs = (rows, rows, P()) + weights + (P(), P(), rows)
    out_specs = (rows, rows, rows) + weights + (P(), P())
    return jax.shard_map(local, mesh=mesh, in_specs=in_specs, out_specs=out_specs, check_vma=False)
```
